512 devices in a mesh: dom: 128 (over z, y, core), mp: 4 (over x).
Axes of the slice: x: 4, y: 8, z: 8, core: 2. Of those that a mesh axis runs over, the one named last changes fastest.
Arguments:
- vertex_embeddings: bfloat16 [32768, 512], P('dom', 'mp'), may hold values from -6 to 6
- upstream_sensitivity: bfloat16 [32768, 512], P('dom', 'mp'), may hold values from -6 to 6
- asking_projector_matrix: bfloat16 [512, 512], P(None, 'mp'), may hold values from -0.25 to 0.25
- lookup_projector_matrix: bfloat16 [512, 512], P(None, 'mp'), may hold values from -0.25 to 0.25
- content_projector_matrix: bfloat16 [512, 512], P(None, 'mp'), may hold values from -0.25 to 0.25
- channel_logit_scales: float32 [8], P('mp'), may hold values from 2 to 8
- adjacent_block_table: int32 [256, 8], P('dom'), may hold values from 0 to 255, as said below
- compressed_link_bitmap: int32 [256, 9, 1024], P('dom'), may hold values from 0 to 65535, as said below
Outputs:
- attended: bfloat16 [32768, 512], P('dom', 'mp')
- input_grad: bfloat16 [32768, 512], P('dom', 'mp')
- grad_query: float32 [512, 512], P(None, 'mp')
- grad_key: float32 [512, 512], P(None, 'mp')
- grad_value: float32 [512, 512], P(None, 'mp')
The draws below stay inside these ranges and needn't reach their ends.
Inputs may be any that keep to these rules, and one draw needn't show every extreme that they name: `adjacent_block_table`: consecutive groups of 2 blocks form partitions. Every block listed for a block lies in its own partition or in the partition just before or just after it. All blocks of one partition that list blocks of the partition before (after) it list the same block of it. The first listed block lies in the partition before and the second in the partition after, where those exist, else in the own partition. `compressed_link_bitmap`: each word holds 16 edge bits of one tile in its lowest bits. Tile 0 of each block has every diagonal edge. For each block, the tiles of its first two or more listed neighbours may hold edges and the tiles after them have none.
All inputs are finite; a program needn't handle non-finite values.
Results may differ from the reference program's by a relative error of at most 0.017.
Values may be sent and summed in bfloat16 or wider, within the bound.
No kernel may reach another device: no remote copies, remote signals or barrier semaphores. Data moves between devices by JAX's collectives and lax.ppermute only.
A program may use at most 64 MiB of HBM per device.

```python
import math
import jax
import jax.numpy as jnp
from jax import lax

D = 512
FOCUS_CHANNELS = 8
CHANNEL_DIM = 64
BLOCK = 128
SLOTS = 8
BLK_DEV = 2
NBLK = 256
NODES = 32768
WORDS = 1024
N_DOM = 128


def neighbour_plan(key):
    key_side, key_left, key_right, key_own, key_first, key_second = jax.random.split(key, 6)
    part_owner = jnp.arange(NBLK, dtype=jnp.int32) // BLK_DEV
    facing = jax.random.randint(key_side, (NBLK, SLOTS), -1, 2)
    facing = facing.at[:, 0].set(-1).at[:, 1].set(1)
    facing = jnp.where((facing < 0) & (part_owner[:, None] == 0), 0, facing)
    facing = jnp.where((facing > 0) & (part_owner[:, None] == N_DOM - 1), 0, facing)
    left_pick = jax.random.randint(key_left, (N_DOM,), 0, BLK_DEV)
    right_pick = jax.random.randint(key_right, (N_DOM,), 0, BLK_DEV)
    own_pick = jax.random.randint(key_own, (NBLK, SLOTS), 0, BLK_DEV)
    within = jnp.where(facing < 0, left_pick[part_owner][:, None], jnp.where(facing > 0, right_pick[part_owner][:, None], own_pick))
    block_ids = (part_owner[:, None] + facing) * BLK_DEV + within
    degree = 2 + jnp.minimum(jax.random.randint(key_first, (NBLK,), 0, SLOTS - 1), jax.random.randint(key_second, (NBLK,), 0, SLOTS - 1))
    return (block_ids.astype(jnp.int32), degree)


def draw_adjacent_block_table(key, part):
    block_ids, degree = neighbour_plan(key)
    return block_ids


def draw_compressed_link_bitmap(key, part):
    block_ids, degree = neighbour_plan(key)
    key = jax.random.fold_in(key, 11)
    key_density, key_edges = jax.random.split(key)
    density = jax.random.randint(key_density, (NBLK, SLOTS + 1, 1, 1), 4, 40)
    raw_edges = jax.random.randint(key_edges, (NBLK, SLOTS + 1, BLOCK, BLOCK), 0, 64) < density
    slot_number = jnp.arange(SLOTS + 1)
    diagonal = jnp.arange(BLOCK)[:, None] == jnp.arange(BLOCK)[None, :]
    raw_edges = raw_edges | (slot_number[None, :, None, None] == 0) & diagonal[None, None]
    live_slot = (slot_number[None, :] == 0) | (slot_number[None, :] - 1 < degree[:, None])
    edges = (raw_edges & live_slot[:, :, None, None]).astype(jnp.int32)
    edges = edges.reshape(NBLK, SLOTS + 1, WORDS, 16)
    bit_value = jnp.left_shift(jnp.ones((16,), jnp.int32), jnp.arange(16, dtype=jnp.int32))
    return jnp.sum(edges * bit_value, axis=-1, dtype=jnp.int32)


def block_levels(key, extent, cuts, smallest, high):
    factor_of = 1.0
    for position, blocks in cuts:
        steps = jax.random.uniform(jax.random.fold_in(jax.random.fold_in(key, 6), position), (blocks,), jnp.float32, smallest / len(cuts), high / len(cuts))
        factor_of = factor_of * jnp.repeat(jnp.exp(steps), extent[position] // blocks).reshape((-1,) + (1,) * (len(extent) - 1 - position))
    return factor_of


def centred(key, extent, width, bound, cuts=(), kind=jnp.bfloat16):
    array = jax.random.normal(key, extent, jnp.float32) * width
    if len(cuts) > 0:
        array = block_levels(key, extent, cuts, -0.22, 0.18) * array
    return jnp.clip(array, min=-bound, max=bound).astype(kind)


def setup_inputs(seed: int = 0) -> dict:
    keys = jax.random.split(jax.random.key(seed), 9)
    vertex_embeddings = centred(keys[0], (NODES, D), 1.0, 6.0, ((0, 128), (1, 4)))
    upstream_sensitivity = centred(keys[1], (NODES, FOCUS_CHANNELS * CHANNEL_DIM), 1.0, 6.0, ((0, 128), (1, 4)))
    asking_projector_matrix = centred(keys[2], (D, FOCUS_CHANNELS * CHANNEL_DIM), D ** -0.5, 0.25, ((1, 4),))
    lookup_projector_matrix = centred(keys[3], (D, FOCUS_CHANNELS * CHANNEL_DIM), D ** -0.5, 0.25, ((1, 4),))
    content_projector_matrix = centred(keys[4], (D, FOCUS_CHANNELS * CHANNEL_DIM), D ** -0.5, 0.25, ((1, 4),))
    channel_logit_scales = jnp.clip(jnp.exp(math.log(8.0) - 1.3862944 * jax.random.uniform(keys[5], (FOCUS_CHANNELS,), jnp.float32) ** block_levels(keys[5], (FOCUS_CHANNELS,), ((0, 4),), -0.2, 0.2)), 2.0, 8.0)
    adjacent_block_table = draw_adjacent_block_table(jax.random.fold_in(keys[8], 71), 0)
    compressed_link_bitmap = draw_compressed_link_bitmap(jax.random.fold_in(keys[8], 71), 0)
    return dict(vertex_embeddings=vertex_embeddings, upstream_sensitivity=upstream_sensitivity, asking_projector_matrix=asking_projector_matrix, lookup_projector_matrix=lookup_projector_matrix, content_projector_matrix=content_projector_matrix, channel_logit_scales=channel_logit_scales, adjacent_block_table=adjacent_block_table, compressed_link_bitmap=compressed_link_bitmap)


epsilon = 1e-06

def head_norm(projected):
    head_split = projected.reshape(projected.shape[0], FOCUS_CHANNELS, CHANNEL_DIM)
    scale_rows = lax.rsqrt(lax.optimization_barrier(jnp.mean(head_split * head_split, axis=-1, keepdims=True)) + epsilon)
    return (head_split * scale_rows, scale_rows)

def norm_back(upstream, unit_vec, scale_rows):
    return scale_rows * (upstream - unit_vec * lax.optimization_barrier(jnp.mean(upstream * unit_vec, axis=-1, keepdims=True)))

def rounded(values):
    return lax.optimization_barrier(values.astype(jnp.bfloat16)).astype(jnp.float32)

def unpack_edges(words):
    bit_place = jnp.arange(16, dtype=jnp.int32)
    bits = jnp.right_shift(words.astype(jnp.int32)[..., None], bit_place) & 1
    return bits.reshape(words.shape[:-1] + (BLOCK, BLOCK))

def reference(vertex_embeddings, upstream_sensitivity, asking_projector_matrix, lookup_projector_matrix, content_projector_matrix, channel_logit_scales, adjacent_block_table, compressed_link_bitmap):
    block_count = adjacent_block_table.shape[0]
    feat_width = FOCUS_CHANNELS * CHANNEL_DIM
    query_proj = jnp.dot(vertex_embeddings, asking_projector_matrix, preferred_element_type=jnp.float32)
    key_proj = jnp.dot(vertex_embeddings, lookup_projector_matrix, preferred_element_type=jnp.float32)
    value_proj = jnp.dot(vertex_embeddings, content_projector_matrix, preferred_element_type=jnp.float32)
    query_unit, query_scale = head_norm(query_proj)
    key_unit, key_scale = head_norm(key_proj)
    query_round = query_unit.astype(jnp.bfloat16).reshape(block_count, BLOCK, FOCUS_CHANNELS, CHANNEL_DIM)
    key_round = key_unit.astype(jnp.bfloat16).reshape(block_count, BLOCK, FOCUS_CHANNELS, CHANNEL_DIM)
    value_round = value_proj.astype(jnp.bfloat16).reshape(block_count, BLOCK, FOCUS_CHANNELS, CHANNEL_DIM)
    logit_scaling_factor = channel_logit_scales.astype(jnp.float32) / CHANNEL_DIM
    tile_list = jnp.concatenate([jnp.arange(block_count, dtype=jnp.int32)[:, None], adjacent_block_table.astype(jnp.int32)], axis=1)
    grad_attn = upstream_sensitivity.reshape(block_count, BLOCK, FOCUS_CHANNELS, CHANNEL_DIM)

    def weights_of(block_index):
        tiles_read = tile_list[block_index]
        key_tiles = jnp.take(key_round, tiles_read, axis=0).astype(jnp.float32)
        value_tiles = jnp.take(value_round, tiles_read, axis=0).astype(jnp.float32)
        query = query_round[block_index].astype(jnp.float32)
        scores = jnp.einsum('qhd,tkhd->htqk', query, key_tiles) * logit_scaling_factor[:, None, None, None]
        live_mask = unpack_edges(compressed_link_bitmap[block_index])[None] != 0
        exp_scores = jnp.where(live_mask, jnp.exp(scores), 0.0)
        row_total = lax.optimization_barrier(jnp.sum(exp_scores, axis=(1, 3), keepdims=True))
        return (tiles_read, key_tiles, value_tiles, query, exp_scores / row_total)

    def forward_block(block_index):
        tiles_read, key_tiles, value_tiles, query, weights = weights_of(block_index)
        return jnp.einsum('htqk,tkhd->qhd', rounded(weights), value_tiles).astype(jnp.bfloat16)
    attended = lax.map(forward_block, jnp.arange(block_count, dtype=jnp.int32)).reshape(NODES, feat_width)

    def backward_block(carried, block_index):
        key_accum, value_accum = carried
        tiles_read, key_tiles, value_tiles, query, weights = weights_of(block_index)
        upstream = grad_attn[block_index].astype(jnp.float32)
        weights_round = rounded(weights)
        grad_weights = jnp.einsum('qhd,tkhd->htqk', upstream, value_tiles)
        row_delta = lax.optimization_barrier(jnp.sum(weights * grad_weights, axis=(1, 3), keepdims=True))
        grad_scores = rounded(weights * (grad_weights - row_delta))
        grad_qn = jnp.einsum('htqk,tkhd->qhd', grad_scores, key_tiles) * logit_scaling_factor[None, :, None]
        grad_kn = jnp.einsum('htqk,qhd->tkhd', grad_scores, query) * logit_scaling_factor[None, None, :, None]
        grad_vn = jnp.einsum('htqk,qhd->tkhd', weights_round, upstream)
        key_accum = key_accum.at[tiles_read].add(grad_kn)
        value_accum = value_accum.at[tiles_read].add(grad_vn)
        return ((key_accum, value_accum), grad_qn)
    empty = jnp.zeros((block_count, BLOCK, FOCUS_CHANNELS, CHANNEL_DIM), jnp.float32)
    (key_accum, value_accum), grad_qs = lax.scan(backward_block, (empty, empty), jnp.arange(block_count, dtype=jnp.int32))
    grad_q = norm_back(grad_qs.reshape(NODES, FOCUS_CHANNELS, CHANNEL_DIM), query_unit, query_scale).reshape(NODES, feat_width).astype(jnp.bfloat16)
    grad_k = norm_back(key_accum.reshape(NODES, FOCUS_CHANNELS, CHANNEL_DIM), key_unit, key_scale).reshape(NODES, feat_width).astype(jnp.bfloat16)
    grad_v = value_accum.reshape(NODES, feat_width).astype(jnp.bfloat16)
    input_sum = jnp.dot(grad_q, asking_projector_matrix.T, preferred_element_type=jnp.float32)
    input_sum = input_sum + jnp.dot(grad_k, lookup_projector_matrix.T, preferred_element_type=jnp.float32)
    input_sum = input_sum + jnp.dot(grad_v, content_projector_matrix.T, preferred_element_type=jnp.float32)
    input_grad = input_sum.astype(jnp.bfloat16)
    grad_scale = NODES ** (-0.5)
    grad_query = jnp.dot(vertex_embeddings.T, grad_q, preferred_element_type=jnp.float32) * grad_scale
    grad_key = jnp.dot(vertex_embeddings.T, grad_k, preferred_element_type=jnp.float32) * grad_scale
    grad_value = jnp.dot(vertex_embeddings.T, grad_v, preferred_element_type=jnp.float32) * grad_scale
    return (attended, input_grad, grad_query, grad_key, grad_value)
```

```python
import jax
import jax.numpy as jnp
from jax import lax
from jax.sharding import PartitionSpec as P

epsilon = 1e-06


def extended_2(cells, sides, width):
    for axis, dim in sides:
        count = lax.axis_size(axis)
        ends = count - 1
        head = lax.slice_in_dim(cells, 0, width, axis=dim)
        tail = lax.slice_in_dim(cells, cells.shape[dim] - width, cells.shape[dim], axis=dim)
        cells = jnp.concatenate(
            [
                lax.ppermute(tail, axis, [(i, (i + 1) % count) for i in range(ends)]),
                cells,
                lax.ppermute(head, axis, [((i + 1) % count, i) for i in range(ends)]),
            ],
            axis=dim,
        )
    return cells


def from_behind(value, axis, steps):
    count = lax.axis_size(axis)
    leading, last = (max(0, -steps), min(count, count - steps))
    return lax.ppermute(value, axis, [(source, source + steps) for source in range(leading, last)])


def head_norm(projected, resident_channels):
    head_split = projected.reshape(projected.shape[0], resident_channels, -1)
    scale_rows = lax.rsqrt(jnp.mean(head_split * head_split, axis=-1, keepdims=True) + epsilon)
    return (head_split * scale_rows, scale_rows)


def norm_back(upstream, unit_vec, scale_rows):
    return scale_rows * (
        upstream - unit_vec * jnp.mean(upstream * unit_vec, axis=-1, keepdims=True)
    )


def spread(value, axis, groups, count):
    copies = jnp.broadcast_to(value[None], (count,) + value.shape)
    return lax.all_to_all(copies, axis, 0, 0, tiled=True, axis_index_groups=groups)


def sum_over_dom(term, part_count):
    rows, columns = term.shape
    half, peers = rows // 2, part_count // 2
    core = lax.axis_index("dom") % 2
    pairs = [(i, i ^ 1) for i in range(part_count)]
    groups = [[2 * i + c for i in range(peers)] for c in range(2)]
    away = lax.dynamic_slice_in_dim(term, (1 - core) * half, half, axis=0).astype(jnp.bfloat16)
    keep = lax.dynamic_slice_in_dim(term, core * half, half, axis=0)
    keep = keep + lax.ppermute(away, "dom", pairs).astype(jnp.float32)
    tall = jnp.concatenate([keep[:, i : i + 128] for i in range(0, columns, 128)], axis=0)
    pieces = tall.astype(jnp.bfloat16).reshape(peers, -1, 128)
    got = lax.all_to_all(pieces, "dom", 0, 0, tiled=True, axis_index_groups=groups)
    mine = jnp.sum(got.astype(jnp.float32), axis=0).astype(jnp.bfloat16)
    tall = spread(mine, "dom", groups, peers).reshape(-1, 128)
    keep = jnp.concatenate(
        [tall[i * half : (i + 1) * half] for i in range(columns // 128)], axis=1
    )
    other = lax.ppermute(keep, "dom", pairs)
    low = jnp.where(core == 0, keep, other)
    high = jnp.where(core == 0, other, keep)
    return jnp.concatenate([low, high], axis=0).astype(jnp.float32)


def shards(
    vertex_embeddings,
    upstream_sensitivity,
    asking_projector_matrix,
    lookup_projector_matrix,
    content_projector_matrix,
    channel_logit_scales,
    adjacent_block_table,
    compressed_link_bitmap,
):
    blocks_here, slot_count = adjacent_block_table.shape
    row_count = upstream_sensitivity.shape[0]
    block_len = row_count // blocks_here
    feat_width = asking_projector_matrix.shape[1]
    resident_channels = channel_logit_scales.shape[0]
    channel_extent = feat_width // resident_channels
    part_count = lax.axis_size("dom")
    my_part = lax.axis_index("dom")
    gathered = spread(vertex_embeddings, "mp", None, lax.axis_size("mp"))
    gathered = jnp.concatenate([gathered[i] for i in range(gathered.shape[0])], axis=1)
    w_joint = jnp.concatenate(
        [asking_projector_matrix, lookup_projector_matrix, content_projector_matrix], axis=1
    )
    projected = jnp.dot(gathered, w_joint, preferred_element_type=jnp.float32)
    query_unit, query_scale = head_norm(projected[:, :feat_width], resident_channels)
    key_unit, key_scale = head_norm(projected[:, feat_width : 2 * feat_width], resident_channels)
    query_round = query_unit.astype(jnp.bfloat16).reshape(
        blocks_here, block_len, resident_channels, channel_extent
    )
    own_kv = jnp.concatenate(
        [
            key_unit.reshape(row_count, feat_width).astype(jnp.bfloat16),
            projected[:, 2 * feat_width :].astype(jnp.bfloat16),
        ],
        axis=1,
    )
    logit_scaling_factor = channel_logit_scales / channel_extent
    offset = adjacent_block_table // blocks_here - my_part
    within = adjacent_block_table % blocks_here
    local_order = jnp.arange(blocks_here, dtype=jnp.int32)
    extended = extended_2(own_kv, (("dom", 0),), row_count)
    extended = extended.reshape(3 * blocks_here, block_len, 2 * feat_width)
    position = (offset + 1) * blocks_here + within
    own_position = blocks_here + local_order
    tile_pos = jnp.concatenate([own_position[:, None], position], axis=1)
    tile_data = jnp.take(extended, tile_pos.reshape(-1), axis=0).reshape(
        blocks_here, slot_count + 1, block_len, 2 * feat_width
    )
    key_tiles = tile_data[..., :feat_width].reshape(
        blocks_here, slot_count + 1, block_len, resident_channels, channel_extent
    )
    value_tiles = tile_data[..., feat_width:].reshape(
        blocks_here, slot_count + 1, block_len, resident_channels, channel_extent
    )
    bit_place = jnp.arange(16, dtype=jnp.int32)
    edge_bits = jnp.right_shift(compressed_link_bitmap[..., None], bit_place) & 1
    edge_bits = edge_bits.reshape(blocks_here, slot_count + 1, block_len, block_len)
    scores = jnp.einsum(
        "bqhd,btkhd->bhtqk", query_round, key_tiles, preferred_element_type=jnp.float32
    )
    scores = scores * logit_scaling_factor[None, :, None, None, None]
    live_mask = (edge_bits != 0)[:, None]
    exp_scores = jnp.where(live_mask, jnp.exp(scores), 0.0)
    row_total = jnp.sum(exp_scores, axis=(2, 4), keepdims=True)
    weights = exp_scores / row_total
    weights_round = weights.astype(jnp.bfloat16)
    attended = jnp.einsum(
        "bhtqk,btkhd->bqhd", weights_round, value_tiles, preferred_element_type=jnp.float32
    )
    attended = attended.astype(jnp.bfloat16).reshape(row_count, feat_width)
    grad_attn = upstream_sensitivity.reshape(
        blocks_here, block_len, resident_channels, channel_extent
    )
    grad_weights = jnp.einsum(
        "bqhd,btkhd->bhtqk", grad_attn, value_tiles, preferred_element_type=jnp.float32
    )
    row_delta = jnp.sum(weights * grad_weights, axis=(2, 4), keepdims=True)
    grad_scores = (weights * (grad_weights - row_delta)).astype(jnp.bfloat16)
    grad_qn = jnp.einsum(
        "bhtqk,btkhd->bqhd", grad_scores, key_tiles, preferred_element_type=jnp.float32
    )
    grad_qn = grad_qn * logit_scaling_factor[None, None, :, None]
    grad_kn = jnp.einsum(
        "bhtqk,bqhd->btkhd", grad_scores, query_round, preferred_element_type=jnp.float32
    )
    grad_kn = grad_kn * logit_scaling_factor[None, None, None, :, None]
    grad_value = jnp.einsum(
        "bhtqk,bqhd->btkhd", weights_round, grad_attn, preferred_element_type=jnp.float32
    )
    tile_grads = jnp.concatenate(
        [
            grad_kn.reshape(blocks_here, slot_count + 1, block_len, feat_width),
            grad_value.reshape(blocks_here, slot_count + 1, block_len, feat_width),
        ],
        axis=-1,
    )
    tile_grads = tile_grads.reshape(blocks_here * (slot_count + 1), block_len * 2 * feat_width)
    ext_grads = (
        jnp.zeros((extended.shape[0], block_len * 2 * feat_width), jnp.float32)
        .at[tile_pos.reshape(-1)]
        .add(tile_grads)
    )
    own_grads = ext_grads[blocks_here : 2 * blocks_here]
    for facing in (-1, 1):
        rim_piece = ext_grads[:blocks_here] if facing == -1 else ext_grads[2 * blocks_here :]
        own_grads = own_grads + from_behind(rim_piece.astype(jnp.bfloat16), "dom", facing).astype(
            rim_piece.dtype
        )
    summed = own_grads.reshape(row_count, 2 * feat_width)
    grad_q = norm_back(
        grad_qn.reshape(row_count, resident_channels, channel_extent), query_unit, query_scale
    ).reshape(row_count, feat_width)
    grad_k = norm_back(
        summed[:, :feat_width].reshape(row_count, resident_channels, channel_extent),
        key_unit,
        key_scale,
    ).reshape(row_count, feat_width)
    grads_joint = jnp.concatenate([grad_q, grad_k, summed[:, feat_width:]], axis=1).astype(
        jnp.bfloat16
    )
    input_part = jnp.einsum("rc,dc->rd", grads_joint, w_joint, preferred_element_type=jnp.float32)
    input_grad = lax.psum_scatter(
        input_part.astype(jnp.bfloat16), "mp", scatter_dimension=1, tiled=True
    )
    grad_scale = (part_count * row_count) ** (-0.5)
    weight_term = jnp.einsum("rd,rc->dc", gathered, grads_joint, preferred_element_type=jnp.float32)
    weight_total = sum_over_dom(weight_term, part_count) * grad_scale
    grad_query = weight_total[:, :feat_width]
    grad_key = weight_total[:, feat_width : 2 * feat_width]
    grad_value_out = weight_total[:, 2 * feat_width :]
    return (attended, input_grad, grad_query, grad_key, grad_value_out)


def solution(mesh):
    in_specs = (
        P("dom", "mp"),
        P("dom", "mp"),
        P(None, "mp"),
        P(None, "mp"),
        P(None, "mp"),
        P("mp"),
        P("dom", None),
        P("dom", None, None),
    )
    out_specs = (P("dom", "mp"), P("dom", "mp"), P(None, "mp"), P(None, "mp"), P(None, "mp"))
    return jax.shard_map(shards, mesh=mesh, in_specs=in_specs, out_specs=out_specs, check_vma=False)
```

```python
import jax
import jax.numpy as jnp
from jax import lax
from jax.experimental import pallas as pl
from jax.experimental.pallas import tpu as pltpu
from jax.sharding import PartitionSpec as P

EPS = 1e-06
F32 = jnp.float32
BF16 = jnp.bfloat16
LANES = 128
VMEM = pl.BlockSpec(memory_space=pltpu.VMEM)
SMEM = pl.BlockSpec(memory_space=pltpu.SMEM)
NN = (((1,), (0,)), ((), ()))
NT = (((1,), (1,)), ((), ()))
TN = (((0,), (0,)), ((), ()))


def mul(a, b, dims=NN):
    return lax.dot_general(a, b, dims, preferred_element_type=F32)


def call(kernel, out, in_specs, scratch=(), flops=0, moved=0):
    return pl.pallas_call(
        kernel,
        out_shape=out,
        in_specs=in_specs,
        out_specs=jax.tree.map(lambda _: VMEM, out),
        scratch_shapes=list(scratch),
        compiler_params=pltpu.CompilerParams(vmem_limit_bytes=40 * 1024 * 1024),
        cost_estimate=pl.CostEstimate(flops=flops, bytes_accessed=moved, transcendentals=0),
    )


def shape(dims, kind):
    return jax.ShapeDtypeStruct(dims, kind)


def count_kernel(place_ref, words_ref, count_ref, total):
    blocks, tiles, words = words_ref.shape
    block = LANES
    per_row = words // block
    rows = block // per_row * 1
    total[...] = jnp.zeros_like(total)
    lane = lax.broadcasted_iota(jnp.int32, (block, block), 1)
    row = lax.broadcasted_iota(jnp.int32, (block, block), 0)
    same = (row % per_row) == (lane // 16)
    low_pick = jnp.where(same & (lane % 16 < 8), 1.0, 0.0)
    high_pick = jnp.where(same & (lane % 16 >= 8), 1.0, 0.0)
    pick = jnp.concatenate([low_pick, high_pick], axis=0).astype(BF16)
    mine = (row[:rows] == lane[:rows] // per_row).astype(F32)
    shift = lane % 8
    for b in range(blocks):
        for t in range(tiles):
            line = words_ref[b, t : t + 1, :]
            low = (line & 255).astype(F32)
            high = lax.shift_right_logical(line, 8).astype(F32)
            spread_rows = []
            for r in range(per_row):
                at = slice(r * block, (r + 1) * block)
                spread_rows.append(
                    jnp.concatenate([low[:, at] * mine, high[:, at] * mine], axis=1)
                )
            wide = jnp.concatenate(spread_rows, axis=0).astype(BF16)
            byte = mul(wide, pick).astype(jnp.int32)
            bits = (lax.shift_right_logical(byte, shift) & 1).astype(F32)
            place = place_ref[b, t]
            total[b, place] = total[b, place] + bits
    for b in range(blocks):
        for s in range(4):
            count_ref[b * block : (b + 1) * block, s * block : (s + 1) * block] = total[
                b, s
            ].astype(BF16)


def head_mean(value, mixer):
    high = value.astype(BF16)
    low = (value - high.astype(F32)).astype(BF16)
    return mul(high, mixer) + mul(low, mixer)


def attend_kernel(
    info_ref,
    scale_ref,
    x_ref,
    xa_ref,
    xb_ref,
    wq_ref,
    wk_ref,
    wv_ref,
    up_ref,
    count_ref,
    att_ref,
    gq_ref,
    gown_ref,
    back_a_ref,
    back_b_ref,
    keep_ref,
    away_ref,
    x_all,
    dw,
):
    core, before, after = info_ref[0], info_ref[1], info_ref[2]
    n = LANES
    for i in range(4):
        x_all[0 : 2 * n, i * n : (i + 1) * n] = x_ref[i]

    @pl.when(core == 0)
    def _():
        for i in range(4):
            x_all[2 * n : 3 * n, i * n : (i + 1) * n] = xb_ref[i, pl.ds(before * n, n), :]
            x_all[3 * n : 4 * n, i * n : (i + 1) * n] = xa_ref[i, pl.ds(after * n, n), :]

    @pl.when(core != 0)
    def _():
        for i in range(4):
            x_all[2 * n : 3 * n, i * n : (i + 1) * n] = xa_ref[i, pl.ds(before * n, n), :]
            x_all[3 * n : 4 * n, i * n : (i + 1) * n] = xb_ref[i, pl.ds(after * n, n), :]

    x = x_all[...]
    q = mul(x[: 2 * n], wq_ref[...])
    k = mul(x, wk_ref[...])
    v = mul(x, wv_ref[...])
    mixer = jnp.where(
        lax.broadcasted_iota(jnp.int32, (n, n), 0) // 64
        == lax.broadcasted_iota(jnp.int32, (n, n), 1) // 64,
        1.0 / 64,
        0.0,
    ).astype(BF16)
    q_scale = lax.rsqrt(head_mean(q * q, mixer) + EPS)
    k_scale = lax.rsqrt(head_mean(k * k, mixer) + EPS)
    q_unit, k_unit = q * q_scale, k * k_scale
    q_round, k_round, v_round = q_unit.astype(BF16), k_unit.astype(BF16), v.astype(BF16)
    up = up_ref[...]
    first = lax.broadcasted_iota(jnp.int32, (1, n), 1) < 64
    heads = [first.astype(F32).astype(BF16), (1 - first.astype(F32)).astype(BF16)]
    factors = [scale_ref[0] / 64, scale_ref[1] / 64]
    lane_factor = jnp.where(first, factors[0], factors[1])
    att, gq = [], []
    gk = jnp.zeros((4 * n, n), F32)
    gv = jnp.zeros((4 * n, n), F32)
    for b in range(2):
        at = slice(b * n, (b + 1) * n)
        count = count_ref[at, :].astype(F32)
        att_b = jnp.zeros((n, n), F32)
        gq_b = jnp.zeros((n, n), F32)
        for h in range(2):
            q_h = q_round[at] * heads[h]
            up_h = up[at] * heads[h]
            scores = mul(q_h, k_round, NT) * factors[h]
            w = count * jnp.exp(scores)
            w = w * (1.0 / jnp.sum(w, axis=1, keepdims=True))
            gw = mul(up_h, v_round, NT)
            delta = jnp.sum(w * gw, axis=1, keepdims=True)
            gs = (w * (gw - delta)).astype(BF16)
            w_round = w.astype(BF16)
            att_b += mul(w_round, v_round * heads[h])
            gq_b += mul(gs, k_round * heads[h])
            gk += mul(gs, q_h, TN)
            gv += mul(w_round, up_h, TN)
        att.append(att_b)
        gq.append(gq_b)
    att_ref[...] = jnp.concatenate(att, axis=0).astype(BF16)
    gqn = jnp.concatenate(gq, axis=0) * lane_factor
    gkn = gk * lane_factor
    gq = (q_scale * (gqn - q_unit * head_mean(gqn * q_unit, mixer))).astype(BF16)
    gk = k_scale * (gkn - k_unit * head_mean(gkn * k_unit, mixer))
    gq_ref[...] = gq
    gown_ref[:, :n] = gk[: 2 * n]
    gown_ref[:, n:] = gv[: 2 * n]
    gk_round, gv_round = gk.astype(BF16), gv.astype(BF16)
    dw[:, :n] = mul(x[: 2 * n], gq, TN)
    dw[:, n : 2 * n] = mul(x, gk_round, TN)
    dw[:, 2 * n :] = mul(x, gv_round, TN)
    sides = [
        (jnp.concatenate([gk_round[s], gv_round[s]], axis=1), which)
        for s, which in ((slice(2 * n, 3 * n), before), (slice(3 * n, 4 * n), after))
    ]

    def put(ref, side):
        ref[:n] = side[0]
        ref[n:] = jnp.full((16, 2 * n), side[1], jnp.int32).astype(F32).astype(BF16)

    @pl.when(core == 0)
    def _():
        put(back_a_ref, sides[1])
        put(back_b_ref, sides[0])

    @pl.when(core != 0)
    def _():
        put(back_a_ref, sides[0])
        put(back_b_ref, sides[1])

    for j in range(3):
        rows, columns = slice(2 * n * j, 2 * n * (j + 1)), slice(n * j, n * (j + 1))
        keep_ref[rows] = dw[pl.ds(core * 2 * n, 2 * n), columns]
        away_ref[rows] = dw[pl.ds((1 - core) * 2 * n, 2 * n), columns].astype(BF16)


def input_kernel(gq_ref, gown_ref, back_a_ref, back_b_ref, wq_ref, wk_ref, wv_ref, part_ref):
    n = LANES
    g = [gown_ref[:n], gown_ref[n:]]
    for ref in (back_a_ref, back_b_ref):
        body = ref[:n].astype(F32)
        which = ref[n : n + 16].astype(F32)[:1]
        g = [g[0] + body * (1 - which), g[1] + body * which]
    g = jnp.concatenate(g, axis=0).astype(BF16)
    part = mul(gq_ref[...], wq_ref[...], NT)
    part += mul(g[:, :n], wk_ref[...], NT)
    part += mul(g[:, n:], wv_ref[...], NT)
    for i in range(4):
        part_ref[i] = part[:, i * n : (i + 1) * n].astype(BF16)


def final_kernel(grad_scale, core_ref, mine_ref, other_ref, gq_ref, gk_ref, gv_ref):
    n = 2 * LANES
    core = core_ref[0]
    for j, ref in enumerate((gq_ref, gk_ref, gv_ref)):
        rows = slice(n * j, n * (j + 1))
        ref[pl.ds(core * n, n), :] = mine_ref[rows].astype(F32) * grad_scale
        ref[pl.ds((1 - core) * n, n), :] = other_ref[rows].astype(F32) * grad_scale


def spread(value, axis, groups, count):
    copies = jnp.broadcast_to(value[None], (count,) + value.shape)
    return lax.all_to_all(copies, axis, 0, 0, tiled=True, axis_index_groups=groups)


def shards(x, up, wq, wk, wv, scales, table, bitmap):
    parts = lax.axis_size("dom")
    part = lax.axis_index("dom")
    core = part % 2
    pairs = [(i, i ^ 1) for i in range(parts)]
    edges = [(i, i + 1) for i in range(1, parts - 1, 2)]
    edges = edges + [(b, a) for a, b in edges]
    peers = parts // 2
    groups = [[2 * i + c for i in range(peers)] for c in range(2)]

    gathered = spread(x, "mp", None, lax.axis_size("mp"))

    side = table // 2 - part
    place = jnp.where(side == 0, table % 2, jnp.where(side < 0, 2, 3))
    place = jnp.concatenate([jnp.arange(2, dtype=jnp.int32)[:, None], place], axis=1)
    info = jnp.stack([core, table[0, 0] % 2, table[0, 1] % 2]).astype(jnp.int32)
    count = call(
        count_kernel,
        shape((256, 512), BF16),
        [SMEM, VMEM],
        [pltpu.VMEM((2, 4, LANES, LANES), F32)],
        flops=2_000_000_000,
        moved=400_000,
    )(place, bitmap)

    xa = lax.ppermute(gathered, "dom", pairs)
    xb = lax.ppermute(gathered, "dom", edges)
    att, gq, gown, back_a, back_b, keep, away = call(
        attend_kernel,
        (
            shape((256, 128), BF16),
            shape((256, 128), BF16),
            shape((256, 256), F32),
            shape((144, 256), BF16),
            shape((144, 256), BF16),
            shape((768, 128), F32),
            shape((768, 128), BF16),
        ),
        [SMEM, SMEM] + [VMEM] * 8,
        [pltpu.VMEM((512, 512), BF16), pltpu.VMEM((512, 384), F32)],
        flops=5_000_000_000,
        moved=4_000_000,
    )(info, scales, gathered, xa, xb, wq, wk, wv, up, count)

    swapped = lax.ppermute(away, "dom", pairs)
    back_a = lax.ppermute(back_a, "dom", pairs)
    back_b = lax.ppermute(back_b, "dom", edges)
    pieces = (keep + swapped.astype(F32)).astype(BF16).reshape(peers, -1, LANES)
    got = lax.all_to_all(pieces, "dom", 0, 0, tiled=True, axis_index_groups=groups)

    input_part = call(
        input_kernel, shape((4, 256, 128), BF16), [VMEM] * 7, flops=1_000_000_000, moved=1_500_000
    )(gq, gown, back_a, back_b, wq, wk, wv)
    input_parts = lax.all_to_all(input_part, "mp", 0, 0, tiled=True)
    input_grad = jnp.sum(input_parts.astype(F32), axis=0).astype(BF16)

    mine = jnp.sum(got.astype(F32), axis=0).astype(BF16)
    mine = spread(mine, "dom", groups, peers).reshape(-1, LANES)
    other = lax.ppermute(mine, "dom", pairs)
    grad_scale = float(parts * 256) ** -0.5

    def finish(*refs):
        final_kernel(grad_scale, *refs)

    grads = call(
        finish, (shape((512, 128), F32),) * 3, [SMEM, VMEM, VMEM], moved=1_500_000
    )(info[:1], mine, other)
    return (att, input_grad) + tuple(grads)


def solution(mesh):
    in_specs = (
        P("dom", "mp"),
        P("dom", "mp"),
        P(None, "mp"),
        P(None, "mp"),
        P(None, "mp"),
        P("mp"),
        P("dom", None),
        P("dom", None, None),
    )
    out_specs = (P("dom", "mp"), P("dom", "mp"), P(None, "mp"), P(None, "mp"), P(None, "mp"))
    return jax.shard_map(shards, mesh=mesh, in_specs=in_specs, out_specs=out_specs, check_vma=False)
```

```python
import jax
import jax.numpy as jnp
from jax import lax
from jax.experimental import pallas as pl
from jax.experimental.pallas import tpu as pltpu
from jax.sharding import PartitionSpec as P

EPS = 1e-06
F32 = jnp.float32
BF16 = jnp.bfloat16
LANES = 128
VMEM = pl.BlockSpec(memory_space=pltpu.VMEM)
SMEM = pl.BlockSpec(memory_space=pltpu.SMEM)
NN = (((1,), (0,)), ((), ()))
NT = (((1,), (1,)), ((), ()))
TN = (((0,), (0,)), ((), ()))


def mul(a, b, dims=NN):
    return lax.dot_general(a, b, dims, preferred_element_type=F32)


def call(kernel, out, in_specs, scratch=(), flops=0, moved=0):
    return pl.pallas_call(
        kernel,
        out_shape=out,
        in_specs=in_specs,
        out_specs=jax.tree.map(lambda _: VMEM, out),
        scratch_shapes=list(scratch),
        compiler_params=pltpu.CompilerParams(vmem_limit_bytes=40 * 1024 * 1024),
        cost_estimate=pl.CostEstimate(flops=flops, bytes_accessed=moved, transcendentals=0),
    )


def shape(dims, kind):
    return jax.ShapeDtypeStruct(dims, kind)


def count_kernel(place_ref, words_ref, count_ref, total):
    blocks, tiles, words = words_ref.shape
    block = LANES
    per_row = words // block
    rows = block // per_row * 1
    total[...] = jnp.zeros_like(total)
    lane = lax.broadcasted_iota(jnp.int32, (block, block), 1)
    row = lax.broadcasted_iota(jnp.int32, (block, block), 0)
    same = (row % per_row) == (lane // 16)
    low_pick = jnp.where(same & (lane % 16 < 8), 1.0, 0.0)
    high_pick = jnp.where(same & (lane % 16 >= 8), 1.0, 0.0)
    pick = jnp.concatenate([low_pick, high_pick], axis=0).astype(BF16)
    mine = (row[:rows] == lane[:rows] // per_row).astype(F32)
    shift = lane % 8
    for b in range(blocks):
        for t in range(tiles):
            line = words_ref[b, t : t + 1, :]
            low = (line & 255).astype(F32)
            high = lax.shift_right_logical(line, 8).astype(F32)
            spread_rows = []
            for r in range(per_row):
                at = slice(r * block, (r + 1) * block)
                spread_rows.append(
                    jnp.concatenate([low[:, at] * mine, high[:, at] * mine], axis=1)
                )
            wide = jnp.concatenate(spread_rows, axis=0).astype(BF16)
            byte = mul(wide, pick).astype(jnp.int32)
            bits = (lax.shift_right_logical(byte, shift) & 1).astype(F32)
            place = place_ref[b, t]
            total[b, place] = total[b, place] + bits
    for b in range(blocks):
        for s in range(4):
            count_ref[b * block : (b + 1) * block, s * block : (s + 1) * block] = total[
                b, s
            ].astype(BF16)


def head_mean(value, mixer):
    high = value.astype(BF16)
    low = (value - high.astype(F32)).astype(BF16)
    return mul(high, mixer) + mul(low, mixer)


def attend_kernel(
    info_ref,
    scale_ref,
    x_ref,
    xa_ref,
    xb_ref,
    wq_ref,
    wk_ref,
    wv_ref,
    up_ref,
    count_ref,
    att_ref,
    gq_ref,
    gown_ref,
    back_a_ref,
    back_b_ref,
    keep_ref,
    away_ref,
    x_all,
    dw,
    away,
):
    core, before, after = info_ref[0], info_ref[1], info_ref[2]
    n = LANES
    for i in range(4):
        x_all[0 : 2 * n, i * n : (i + 1) * n] = x_ref[i]

    @pl.when(core == 0)
    def _():
        for i in range(4):
            x_all[2 * n : 3 * n, i * n : (i + 1) * n] = xb_ref[i, pl.ds(before * n, n), :]
            x_all[3 * n : 4 * n, i * n : (i + 1) * n] = xa_ref[i, pl.ds(after * n, n), :]

    @pl.when(core != 0)
    def _():
        for i in range(4):
            x_all[2 * n : 3 * n, i * n : (i + 1) * n] = xa_ref[i, pl.ds(before * n, n), :]
            x_all[3 * n : 4 * n, i * n : (i + 1) * n] = xb_ref[i, pl.ds(after * n, n), :]

    x = x_all[...]
    q = mul(x[: 2 * n], wq_ref[...])
    k = mul(x, wk_ref[...])
    v = mul(x, wv_ref[...])
    mixer = jnp.where(
        lax.broadcasted_iota(jnp.int32, (n, n), 0) // 64
        == lax.broadcasted_iota(jnp.int32, (n, n), 1) // 64,
        1.0 / 64,
        0.0,
    ).astype(BF16)
    q_scale = lax.rsqrt(head_mean(q * q, mixer) + EPS)
    k_scale = lax.rsqrt(head_mean(k * k, mixer) + EPS)
    q_unit, k_unit = q * q_scale, k * k_scale
    q_round, k_round, v_round = q_unit.astype(BF16), k_unit.astype(BF16), v.astype(BF16)
    up = up_ref[...]
    first = lax.broadcasted_iota(jnp.int32, (1, n), 1) < 64
    heads = [first.astype(F32).astype(BF16), (1 - first.astype(F32)).astype(BF16)]
    factors = [scale_ref[0] / 64, scale_ref[1] / 64]
    lane_factor = jnp.where(first, factors[0], factors[1])
    att, gq = [], []
    gk = jnp.zeros((4 * n, n), F32)
    gv = jnp.zeros((4 * n, n), F32)
    for b in range(2):
        at = slice(b * n, (b + 1) * n)
        count = count_ref[at, :].astype(F32)
        att_b = jnp.zeros((n, n), F32)
        gq_b = jnp.zeros((n, n), F32)
        for h in range(2):
            q_h = q_round[at] * heads[h]
            up_h = up[at] * heads[h]
            scores = mul(q_h, k_round, NT) * factors[h]
            w = count * jnp.exp(scores)
            w = w * (1.0 / jnp.sum(w, axis=1, keepdims=True))
            gw = mul(up_h, v_round, NT)
            delta = jnp.sum(w * gw, axis=1, keepdims=True)
            gs = (w * (gw - delta)).astype(BF16)
            w_round = w.astype(BF16)
            att_b += mul(w_round, v_round * heads[h])
            gq_b += mul(gs, k_round * heads[h])
            gk += mul(gs, q_h, TN)
            gv += mul(w_round, up_h, TN)
        att.append(att_b)
        gq.append(gq_b)
    att_ref[...] = jnp.concatenate(att, axis=0).astype(BF16)
    gqn = jnp.concatenate(gq, axis=0) * lane_factor
    gkn = gk * lane_factor
    gq = (q_scale * (gqn - q_unit * head_mean(gqn * q_unit, mixer))).astype(BF16)
    gk = k_scale * (gkn - k_unit * head_mean(gkn * k_unit, mixer))
    gq_ref[...] = gq
    gown_ref[:, :n] = gk[: 2 * n]
    gown_ref[:, n:] = gv[: 2 * n]
    gk_round, gv_round = gk.astype(BF16), gv.astype(BF16)
    dw[:, :n] = mul(x[: 2 * n], gq, TN)
    dw[:, n : 2 * n] = mul(x, gk_round, TN)
    dw[:, 2 * n :] = mul(x, gv_round, TN)
    sides = [
        (jnp.concatenate([gk_round[s], gv_round[s]], axis=1), which)
        for s, which in ((slice(2 * n, 3 * n), before), (slice(3 * n, 4 * n), after))
    ]

    def put(ref, side):
        ref[:n] = side[0]
        ref[n:] = jnp.full((16, 2 * n), side[1], jnp.int32).astype(F32).astype(BF16)

    @pl.when(core == 0)
    def _():
        put(back_a_ref, sides[1])
        put(back_b_ref, sides[0])

    @pl.when(core != 0)
    def _():
        put(back_a_ref, sides[0])
        put(back_b_ref, sides[1])

    for ref, half in ((keep_ref, core), (away, 1 - core)):
        for j in range(3):
            for i in range(4):
                rows = pl.ds(pl.multiple_of(half * 2 * n + i * 64, 64), 64)
                ref[:, 4 * j + i, :] = dw[rows, n * j : n * (j + 1)]
    away_ref[...] = away[...].astype(BF16)


def input_kernel(
    member_ref,
    gq_ref,
    gown_ref,
    back_a_ref,
    back_b_ref,
    wq_ref,
    wk_ref,
    wv_ref,
    own_ref,
    one_ref,
    two_ref,
    three_ref,
    pieces,
):
    n = LANES
    g = [gown_ref[:n], gown_ref[n:]]
    for ref in (back_a_ref, back_b_ref):
        body = ref[:n].astype(F32)
        which = ref[n : n + 16].astype(F32)[:1]
        g = [g[0] + body * (1 - which), g[1] + body * which]
    g = jnp.concatenate(g, axis=0).astype(BF16)
    part = mul(gq_ref[...], wq_ref[...], NT)
    part += mul(g[:, :n], wk_ref[...], NT)
    part += mul(g[:, n:], wv_ref[...], NT)
    for i in range(4):
        pieces[i] = part[:, i * n : (i + 1) * n]
    member = member_ref[0]
    own_ref[...] = pieces[member]
    for step, ref in enumerate((one_ref, two_ref, three_ref)):
        ref[...] = pieces[lax.rem(member + step + 1, 4)].astype(BF16)


def copies_kernel(value_ref, out_ref):
    for i in range(out_ref.shape[0]):
        out_ref[i] = value_ref[...]


def total_kernel(got_ref, out_ref):
    total = jnp.sum(got_ref[...].astype(F32), axis=0).astype(BF16)
    out_ref[...] = jnp.broadcast_to(total[None], out_ref.shape)


def add_kernel(own_ref, one_ref, two_ref, three_ref, out_ref):
    total = own_ref[...] + one_ref[...].astype(F32)
    total = total + two_ref[...].astype(F32) + three_ref[...].astype(F32)
    out_ref[...] = total.astype(BF16)


def final_kernel(grad_scale, core_ref, mine_ref, other_ref, gq_ref, gk_ref, gv_ref, wide):
    n = 2 * LANES
    core = core_ref[0]
    for ref, half in ((mine_ref, core), (other_ref, 1 - core)):
        wide[...] = ref[...].astype(F32) * grad_scale
        for j, out in enumerate((gq_ref, gk_ref, gv_ref)):
            for i in range(4):
                rows = pl.ds(pl.multiple_of(half * n + i * 64, 64), 64)
                out[rows, :] = wide[:, 4 * j + i, :]


def merge_kernel(keep_ref, swapped_ref, out_ref):
    out_ref[...] = (keep_ref[...] + swapped_ref[...].astype(F32)).astype(BF16)


def shards(x, up, wq, wk, wv, scales, table, bitmap):
    parts = lax.axis_size("dom")
    part = lax.axis_index("dom")
    core = part % 2
    pairs = [(i, i ^ 1) for i in range(parts)]
    edges = [(i, i + 1) for i in range(1, parts - 1, 2)]
    edges = edges + [(b, a) for a, b in edges]
    peers = parts // 2
    groups = [[2 * i + c for i in range(peers)] for c in range(2)]

    members = lax.axis_size("mp")
    copies = call(copies_kernel, shape((members,) + x.shape, BF16), [VMEM], moved=400_000)(x)
    gathered = lax.all_to_all(copies, "mp", 0, 0, tiled=True)

    side = table // 2 - part
    place = jnp.where(side == 0, table % 2, jnp.where(side < 0, 2, 3))
    place = jnp.concatenate([jnp.arange(2, dtype=jnp.int32)[:, None], place], axis=1)
    info = jnp.stack([core, table[0, 0] % 2, table[0, 1] % 2]).astype(jnp.int32)
    count = call(
        count_kernel,
        shape((256, 512), BF16),
        [SMEM, VMEM],
        [pltpu.VMEM((2, 4, LANES, LANES), F32)],
        flops=2_000_000_000,
        moved=400_000,
    )(place, bitmap)

    gathered, count = lax.optimization_barrier((gathered, count))
    xa = lax.ppermute(gathered, "dom", pairs)
    xb = lax.ppermute(gathered, "dom", edges)
    att, gq, gown, back_a, back_b, keep, away = call(
        attend_kernel,
        (
            shape((256, 128), BF16),
            shape((256, 128), BF16),
            shape((256, 256), F32),
            shape((144, 256), BF16),
            shape((144, 256), BF16),
            shape((64, 12, 128), F32),
            shape((64, 12, 128), BF16),
        ),
        [SMEM, SMEM] + [VMEM] * 8,
        [pltpu.VMEM((512, 512), BF16), pltpu.VMEM((512, 384), F32), pltpu.VMEM((64, 12, 128), F32)],
        flops=5_000_000_000,
        moved=4_000_000,
    )(info, scales, gathered, xa, xb, wq, wk, wv, up, count)

    swapped = lax.ppermute(away, "dom", pairs)
    back_a = lax.ppermute(back_a, "dom", pairs)
    back_b = lax.ppermute(back_b, "dom", edges)
    pieces = call(merge_kernel, shape((64, 12, 128), BF16), [VMEM] * 2, moved=800_000)(
        keep, swapped
    )
    got = lax.all_to_all(pieces, "dom", 0, 0, tiled=True, axis_index_groups=groups)

    totals = call(total_kernel, shape(got.shape, BF16), [VMEM], moved=500_000)(got)
    totals, back_a, back_b = lax.optimization_barrier((totals, back_a, back_b))
    member = lax.axis_index("mp").reshape(1)
    own, one, two, three = call(
        input_kernel,
        (shape((256, 128), F32),) + (shape((256, 128), BF16),) * 3,
        [SMEM] + [VMEM] * 7,
        [pltpu.VMEM((4, 256, 128), F32)],
        flops=20_000_000_000,
        moved=1_500_000,
    )(member, gq, gown, back_a, back_b, wq, wk, wv)
    one, two, three = (
        lax.ppermute(v, "mp", [(i, (i + s) % members) for i in range(members)])
        for s, v in ((1, one), (2, two), (3, three))
    )
    input_grad = call(add_kernel, shape((256, 128), BF16), [VMEM] * 4, moved=400_000)(
        own, one, two, three
    )

    mine = lax.all_to_all(totals, "dom", 0, 0, tiled=True, axis_index_groups=groups)
    mine, input_grad = lax.optimization_barrier((mine, input_grad))
    other = lax.ppermute(mine, "dom", pairs)
    grad_scale = float(parts * 256) ** -0.5

    def finish(*refs):
        final_kernel(grad_scale, *refs)

    grads = call(
        finish, (shape((512, 128), F32),) * 3, [SMEM, VMEM, VMEM], [pltpu.VMEM((64, 12, 128), F32)],
        moved=1_500_000,
    )(info[:1], mine, other)
    return (att, input_grad) + tuple(grads)


def solution(mesh):
    in_specs = (
        P("dom", "mp"),
        P("dom", "mp"),
        P(None, "mp"),
        P(None, "mp"),
        P(None, "mp"),
        P("mp"),
        P("dom", None),
        P("dom", None, None),
    )
    out_specs = (P("dom", "mp"), P("dom", "mp"), P(None, "mp"), P(None, "mp"), P(None, "mp"))
    return jax.shard_map(shards, mesh=mesh, in_specs=in_specs, out_specs=out_specs, check_vma=False)
```

```python
import jax
import jax.numpy as jnp
from jax import lax
from jax.experimental import pallas as pl
from jax.experimental.pallas import tpu as pltpu
from jax.sharding import PartitionSpec as P

EPS = 1e-06
F32 = jnp.float32
BF16 = jnp.bfloat16
LANES = 128
VMEM = pl.BlockSpec(memory_space=pltpu.VMEM)
SMEM = pl.BlockSpec(memory_space=pltpu.SMEM)
NN = (((1,), (0,)), ((), ()))
NT = (((1,), (1,)), ((), ()))
TN = (((0,), (0,)), ((), ()))


def mul(a, b, dims=NN):
    return lax.dot_general(a, b, dims, preferred_element_type=F32)


def call(kernel, out, in_specs, scratch=(), flops=0, moved=0):
    return pl.pallas_call(
        kernel,
        out_shape=out,
        in_specs=in_specs,
        out_specs=jax.tree.map(lambda _: VMEM, out),
        scratch_shapes=list(scratch),
        compiler_params=pltpu.CompilerParams(vmem_limit_bytes=40 * 1024 * 1024),
        cost_estimate=pl.CostEstimate(flops=flops, bytes_accessed=moved, transcendentals=0),
    )


def shape(dims, kind):
    return jax.ShapeDtypeStruct(dims, kind)


def count_kernel(part_ref, table_ref, words_ref, count_ref, total):
    blocks, tiles, words = words_ref.shape
    block = LANES
    per_row = words // block
    rows = block // per_row * 1
    total[...] = jnp.zeros_like(total)
    lane = lax.broadcasted_iota(jnp.int32, (block, block), 1)
    row = lax.broadcasted_iota(jnp.int32, (block, block), 0)
    same = (row % per_row) == (lane // 16)
    low_pick = jnp.where(same & (lane % 16 < 8), 1.0, 0.0)
    high_pick = jnp.where(same & (lane % 16 >= 8), 1.0, 0.0)
    pick = jnp.concatenate([low_pick, high_pick], axis=0).astype(BF16)
    mine = (row[:rows] == lane[:rows] // per_row).astype(F32)
    shift = lane % 8
    for b in range(blocks):
        for t in range(tiles):
            line = words_ref[b, t : t + 1, :]
            low = (line & 255).astype(F32)
            high = lax.shift_right_logical(line, 8).astype(F32)
            spread_rows = []
            for r in range(per_row):
                at = slice(r * block, (r + 1) * block)
                spread_rows.append(
                    jnp.concatenate([low[:, at] * mine, high[:, at] * mine], axis=1)
                )
            wide = jnp.concatenate(spread_rows, axis=0).astype(BF16)
            byte = mul(wide, pick).astype(jnp.int32)
            bits = (lax.shift_right_logical(byte, shift) & 1).astype(F32)
            place = b
            if t > 0:
                block_id = table_ref[b, t - 1]
                side = block_id // 2 - part_ref[0]
                place = jnp.where(side == 0, block_id % 2, jnp.where(side < 0, 2, 3))
            total[b, place] = total[b, place] + bits
    for b in range(blocks):
        for s in range(4):
            count_ref[b * block : (b + 1) * block, s * block : (s + 1) * block] = total[
                b, s
            ].astype(BF16)


def head_mixer():
    n = LANES
    row = lax.broadcasted_iota(jnp.int32, (2 * n, n), 0) % n
    lane = lax.broadcasted_iota(jnp.int32, (2 * n, n), 1)
    return jnp.where(row // 64 == lane // 64, 1.0 / 64, 0.0).astype(BF16)


def head_mean(value, mixer):
    high = value.astype(BF16)
    low = (value - high.astype(F32)).astype(BF16)
    return mul(jnp.concatenate([high, low], axis=1), mixer)


def head_lanes():
    first = lax.broadcasted_iota(jnp.int32, (1, LANES), 1) < 64
    ones = first.astype(F32)
    return first, [ones.astype(BF16), (1 - ones).astype(BF16)]


def own_kernel(
    scale_ref,
    x_ref,
    wq_ref,
    wk_ref,
    wv_ref,
    up_ref,
    count_ref,
    q_unit_ref,
    q_scale_ref,
    k_unit_ref,
    k_scale_ref,
    v_ref,
    e_ref,
    gw_ref,
    x_own,
):
    n = LANES
    for i in range(4):
        x_own[:, i * n : (i + 1) * n] = x_ref[i]
    x = x_own[...]
    mixer = head_mixer()
    first, heads = head_lanes()
    w_kv = jnp.concatenate([wk_ref[...], wv_ref[...]], axis=1)
    kv = mul(x, w_kv)
    q, k = mul(x, wq_ref[...]), kv[:, :n]
    q_scale = lax.rsqrt(head_mean(q * q, mixer) + EPS)
    k_scale = lax.rsqrt(head_mean(k * k, mixer) + EPS)
    q_unit, k_unit = q * q_scale, k * k_scale
    q_unit_ref[...], q_scale_ref[...] = q_unit, q_scale
    k_unit_ref[...], k_scale_ref[...] = k_unit, k_scale
    q_round, k_round, v_round = q_unit.astype(BF16), k_unit.astype(BF16), kv[:, n:].astype(BF16)
    v_ref[...] = v_round
    count = count_ref[:, : 2 * n].astype(F32)
    up = up_ref[...]
    for h in range(2):
        scores = mul(q_round * heads[h], k_round, NT) * (scale_ref[h] / 64)
        e_ref[h] = count * jnp.exp(scores)
        gw_ref[h] = mul(up * heads[h], v_round, NT)


def attend_kernel(
    part_ref,
    table_ref,
    scale_ref,
    x_ref,
    xa_ref,
    xb_ref,
    wk_ref,
    wv_ref,
    up_ref,
    count_ref,
    q_unit_ref,
    q_scale_ref,
    k_unit_ref,
    k_scale_ref,
    v_ref,
    e_ref,
    gw_ref,
    att_ref,
    gq_ref,
    gown_ref,
    back_a_ref,
    back_b_ref,
    pieces_ref,
    x_all,
    dw,
    wide,
    kv_near,
    q_stack,
    up_stack,
    gs_stack,
    w_stack,
):
    core, before, after = part_ref[0] % 2, table_ref[0, 0] % 2, table_ref[0, 1] % 2
    n = LANES
    for i in range(4):
        x_all[0 : 2 * n, i * n : (i + 1) * n] = x_ref[i]

    @pl.when(core == 0)
    def _():
        for i in range(4):
            x_all[2 * n : 3 * n, i * n : (i + 1) * n] = xb_ref[i, pl.ds(before * n, n), :]
            x_all[3 * n : 4 * n, i * n : (i + 1) * n] = xa_ref[i, pl.ds(after * n, n), :]

    @pl.when(core != 0)
    def _():
        for i in range(4):
            x_all[2 * n : 3 * n, i * n : (i + 1) * n] = xa_ref[i, pl.ds(before * n, n), :]
            x_all[3 * n : 4 * n, i * n : (i + 1) * n] = xb_ref[i, pl.ds(after * n, n), :]

    mixer = head_mixer()
    first, heads = head_lanes()
    w_kv = jnp.concatenate([wk_ref[...], wv_ref[...]], axis=1)
    kv_near[...] = mul(x_all[2 * n :], w_kv)
    k = kv_near[:, :n]
    near_scale = lax.rsqrt(head_mean(k * k, mixer) + EPS)
    near_unit = k * near_scale
    k_near, v_near = near_unit.astype(BF16), kv_near[:, n:].astype(BF16)
    k_round = jnp.concatenate([k_unit_ref[...].astype(BF16), k_near], axis=0)
    v_round = jnp.concatenate([v_ref[...], v_near], axis=0)
    q_round, up = q_unit_ref[...].astype(BF16), up_ref[...]
    factors = [scale_ref[0] / 64, scale_ref[1] / 64]
    lane_factor = jnp.where(first, factors[0], factors[1])
    for b in range(2):
        at = slice(b * n, (b + 1) * n)
        count = count_ref[at, 2 * n :].astype(F32)
        for h in range(2):
            put = slice((2 * b + h) * n, (2 * b + h + 1) * n)
            q_h, up_h = q_round[at] * heads[h], up[at] * heads[h]
            q_stack[put], up_stack[put] = q_h, up_h
            far = count * jnp.exp(mul(q_h, k_near, NT) * factors[h])
            own = e_ref[h, at, :]
            total = jnp.sum(own[:, :n] + own[:, n:] + far[:, :n] + far[:, n:], axis=1, keepdims=True)
            inverse = 1.0 / total
            own, far = own * inverse, far * inverse
            gw_own, gw_far = gw_ref[h, at, :], mul(up_h, v_near, NT)
            own_d, far_d = own * gw_own, far * gw_far
            delta = jnp.sum(
                own_d[:, :n] + own_d[:, n:] + far_d[:, :n] + far_d[:, n:], axis=1, keepdims=True
            )
            w_stack[put, : 2 * n], w_stack[put, 2 * n :] = own.astype(BF16), far.astype(BF16)
            gs_stack[put, : 2 * n] = (own_d - own * delta).astype(BF16)
            gs_stack[put, 2 * n :] = (far_d - far * delta).astype(BF16)
    gqn = []
    for b in range(2):
        low, high = slice(2 * b * n, (2 * b + 1) * n), slice((2 * b + 1) * n, (2 * b + 2) * n)
        at = slice(b * n, (b + 1) * n)
        att = jnp.where(first, mul(w_stack[low], v_round), mul(w_stack[high], v_round))
        att_ref[at] = att.astype(BF16)
        gqn.append(jnp.where(first, mul(gs_stack[low], k_round), mul(gs_stack[high], k_round)))
    gqn = jnp.concatenate(gqn, axis=0) * lane_factor
    gkn = mul(gs_stack[...], q_stack[...], TN) * lane_factor
    gv = mul(w_stack[...], up_stack[...], TN)
    q_unit, q_scale = q_unit_ref[...], q_scale_ref[...]
    k_unit = jnp.concatenate([k_unit_ref[...], near_unit], axis=0)
    k_scale = jnp.concatenate([k_scale_ref[...], near_scale], axis=0)
    gq = (q_scale * (gqn - q_unit * head_mean(gqn * q_unit, mixer))).astype(BF16)
    gk = k_scale * (gkn - k_unit * head_mean(gkn * k_unit, mixer))
    gq_ref[...] = gq
    gown_ref[:, :n] = gk[: 2 * n]
    gown_ref[:, n:] = gv[: 2 * n]
    gk_round, gv_round = gk.astype(BF16), gv.astype(BF16)
    dw[:, :n] = mul(x_all[: 2 * n], gq, TN)
    dw[:, n:] = mul(x_all[...], jnp.concatenate([gk_round, gv_round], axis=1), TN)
    for i in range(4):
        lanes = slice((i % 2) * 3 * n, (i % 2 + 1) * 3 * n)
        wide[:, i // 2, lanes] = dw[i * n : (i + 1) * n, :]
    pieces_ref[...] = wide[...].astype(BF16)
    sides = [
        (jnp.concatenate([gk_round[s], gv_round[s]], axis=1), which)
        for s, which in ((slice(2 * n, 3 * n), before), (slice(3 * n, 4 * n), after))
    ]

    def put(ref, side):
        ref[:n] = side[0]
        ref[n:] = jnp.full((16, 2 * n), side[1], jnp.int32).astype(F32).astype(BF16)

    @pl.when(core == 0)
    def _():
        put(back_a_ref, sides[1])
        put(back_b_ref, sides[0])

    @pl.when(core != 0)
    def _():
        put(back_a_ref, sides[0])
        put(back_b_ref, sides[1])


def input_kernel(
    member_ref,
    gq_ref,
    gown_ref,
    back_a_ref,
    back_b_ref,
    wq_ref,
    wk_ref,
    wv_ref,
    own_ref,
    one_ref,
    two_ref,
    three_ref,
    pieces,
):
    n = LANES
    g = [gown_ref[:n], gown_ref[n:]]
    for ref in (back_a_ref, back_b_ref):
        body = ref[:n].astype(F32)
        which = ref[n : n + 16].astype(F32)[:1]
        g = [g[0] + body * (1 - which), g[1] + body * which]
    g = jnp.concatenate(g, axis=0).astype(BF16)
    part = mul(gq_ref[...], wq_ref[...], NT)
    part += mul(g[:, :n], wk_ref[...], NT)
    part += mul(g[:, n:], wv_ref[...], NT)
    for i in range(4):
        pieces[i] = part[:, i * n : (i + 1) * n]
    member = member_ref[0]
    own_ref[...] = pieces[member]
    for step, ref in enumerate((one_ref, two_ref, three_ref)):
        ref[...] = pieces[lax.rem(member + step + 1, 4)].astype(BF16)


def copies_kernel(value_ref, out_ref):
    for i in range(out_ref.shape[0]):
        out_ref[i] = value_ref[...]


def total_kernel(got_ref, out_ref):
    total = jnp.sum(got_ref[...].astype(F32), axis=0).astype(BF16)
    out_ref[...] = jnp.broadcast_to(total[None], out_ref.shape)


def add_kernel(own_ref, one_ref, two_ref, three_ref, out_ref):
    total = own_ref[...] + one_ref[...].astype(F32)
    total = total + two_ref[...].astype(F32) + three_ref[...].astype(F32)
    out_ref[...] = total.astype(BF16)


def final_kernel(grad_scale, mine_ref, gq_ref, gk_ref, gv_ref, wide):
    n = LANES
    wide[...] = mine_ref[...].astype(F32) * grad_scale
    for i in range(4):
        for j, out in enumerate((gq_ref, gk_ref, gv_ref)):
            at = ((i % 2) * 3 + j) * n
            out[i * n : (i + 1) * n, :] = wide[:, i // 2, at : at + n]


def shards(x, up, wq, wk, wv, scales, table, bitmap):
    parts = lax.axis_size("dom")
    part = lax.axis_index("dom")
    pairs = [(i, i ^ 1) for i in range(parts)]
    edges = [(i, i + 1) for i in range(1, parts - 1, 2)]
    edges = edges + [(b, a) for a, b in edges]

    members = lax.axis_size("mp")
    copies = call(copies_kernel, shape((members,) + x.shape, BF16), [VMEM], moved=400_000)(x)
    gathered = lax.all_to_all(copies, "mp", 0, 0, tiled=True)

    part_in = part.astype(jnp.int32).reshape(1)
    count = call(
        count_kernel,
        shape((256, 512), BF16),
        [SMEM, SMEM, VMEM],
        [pltpu.VMEM((2, 4, LANES, LANES), F32)],
        flops=2_000_000_000,
        moved=400_000,
    )(part_in, table, bitmap)

    gathered, count = lax.optimization_barrier((gathered, count))
    xa = lax.ppermute(gathered, "dom", pairs)
    xb = lax.ppermute(gathered, "dom", edges)
    tall = shape((256, 128), F32)
    square = shape((2, 256, 256), F32)
    own_parts = call(
        own_kernel,
        (tall, tall, tall, tall, shape((256, 128), BF16), square, square),
        [SMEM] + [VMEM] * 6,
        [pltpu.VMEM((256, 512), BF16)],
        flops=3_000_000_000,
        moved=3_000_000,
    )(scales, gathered, wq, wk, wv, up, count)
    att, gq, gown, back_a, back_b, pieces = call(
        attend_kernel,
        (
            shape((256, 128), BF16),
            shape((256, 128), BF16),
            shape((256, 256), F32),
            shape((144, 256), BF16),
            shape((144, 256), BF16),
            shape((128, 2, 768), BF16),
        ),
        [SMEM, SMEM, SMEM] + [VMEM] * 14,
        [
            pltpu.VMEM((512, 512), BF16),
            pltpu.VMEM((512, 384), F32),
            pltpu.VMEM((128, 2, 768), F32),
            pltpu.VMEM((256, 256), F32),
            pltpu.VMEM((512, 128), BF16),
            pltpu.VMEM((512, 128), BF16),
            pltpu.VMEM((512, 512), BF16),
            pltpu.VMEM((512, 512), BF16),
        ],
        flops=3_000_000_000,
        moved=4_000_000,
    )(part_in, table, scales, gathered, xa, xb, wk, wv, up, count, *own_parts)

    got = lax.all_to_all(pieces, "dom", 0, 0, tiled=True)
    back_a = lax.ppermute(back_a, "dom", pairs)
    back_b = lax.ppermute(back_b, "dom", edges)
    own, one, two, three = call(
        input_kernel,
        (shape((256, 128), F32),) + (shape((256, 128), BF16),) * 3,
        [SMEM] + [VMEM] * 7,
        [pltpu.VMEM((4, 256, 128), F32)],
        flops=1_000_000_000,
        moved=1_500_000,
    )(lax.axis_index("mp").reshape(1), gq, gown, back_a, back_b, wq, wk, wv)
    got, own, one, two, three = lax.optimization_barrier((got, own, one, two, three))
    totals = call(total_kernel, shape(got.shape, BF16), [VMEM], moved=500_000)(got)
    one, two, three = (
        lax.ppermute(v, "mp", [(i, (i + s) % members) for i in range(members)])
        for s, v in ((1, one), (2, two), (3, three))
    )
    input_grad = call(
        add_kernel, shape((256, 128), BF16), [VMEM] * 4, moved=400_000
    )(own, one, two, three)
    mine = lax.all_to_all(totals, "dom", 0, 0, tiled=True)
    grad_scale = float(parts * 256) ** -0.5

    def finish(*refs):
        final_kernel(grad_scale, *refs)

    grads = call(
        finish,
        (shape((512, 128), F32),) * 3,
        [VMEM],
        [pltpu.VMEM((128, 2, 768), F32)],
        moved=1_500_000,
    )(mine)
    return (att, input_grad) + tuple(grads)


def solution(mesh):
    in_specs = (
        P("dom", "mp"),
        P("dom", "mp"),
        P(None, "mp"),
        P(None, "mp"),
        P(None, "mp"),
        P("mp"),
        P("dom", None),
        P("dom", None, None),
    )
    out_specs = (P("dom", "mp"), P("dom", "mp"), P(None, "mp"), P(None, "mp"), P(None, "mp"))
    return jax.shard_map(shards, mesh=mesh, in_specs=in_specs, out_specs=out_specs, check_vma=False)
```

```python
import jax
import jax.numpy as jnp
from jax import lax
from jax.experimental import pallas as pl
from jax.experimental.pallas import tpu as pltpu
from jax.sharding import PartitionSpec as P

EPS = 1e-06
F32 = jnp.float32
BF16 = jnp.bfloat16
LANES = 128
VMEM = pl.BlockSpec(memory_space=pltpu.VMEM)
SMEM = pl.BlockSpec(memory_space=pltpu.SMEM)
NN = (((1,), (0,)), ((), ()))
NT = (((1,), (1,)), ((), ()))
TN = (((0,), (0,)), ((), ()))


def mul(a, b, dims=NN):
    return lax.dot_general(a, b, dims, preferred_element_type=F32)


def call(kernel, out, in_specs, scratch=(), flops=0, moved=0):
    return pl.pallas_call(
        kernel,
        out_shape=out,
        in_specs=in_specs,
        out_specs=jax.tree.map(lambda _: VMEM, out),
        scratch_shapes=list(scratch),
        compiler_params=pltpu.CompilerParams(vmem_limit_bytes=40 * 1024 * 1024),
        cost_estimate=pl.CostEstimate(flops=flops, bytes_accessed=moved, transcendentals=0),
    )


def shape(dims, kind):
    return jax.ShapeDtypeStruct(dims, kind)


def count_kernel(part_ref, table_ref, words_ref, count_ref, total):
    blocks, tiles, words = words_ref.shape
    block = LANES
    per_row = words // block
    rows = block // per_row * 1
    total[...] = jnp.zeros_like(total)
    lane = lax.broadcasted_iota(jnp.int32, (block, block), 1)
    row = lax.broadcasted_iota(jnp.int32, (block, block), 0)
    same = (row % per_row) == (lane // 16)
    low_pick = jnp.where(same & (lane % 16 < 8), 1.0, 0.0)
    high_pick = jnp.where(same & (lane % 16 >= 8), 1.0, 0.0)
    pick = jnp.concatenate([low_pick, high_pick], axis=0).astype(BF16)
    mine = (row[:rows] == lane[:rows] // per_row).astype(F32)
    shift = lane % 8
    for b in range(blocks):
        for t in range(tiles):
            line = words_ref[b, t : t + 1, :]
            low = (line & 255).astype(F32)
            high = lax.shift_right_logical(line, 8).astype(F32)
            spread_rows = []
            for r in range(per_row):
                at = slice(r * block, (r + 1) * block)
                spread_rows.append(
                    jnp.concatenate([low[:, at] * mine, high[:, at] * mine], axis=1)
                )
            wide = jnp.concatenate(spread_rows, axis=0).astype(BF16)
            byte = mul(wide, pick).astype(jnp.int32)
            bits = (lax.shift_right_logical(byte, shift) & 1).astype(F32)
            place = b
            if t > 0:
                block_id = table_ref[b, t - 1]
                side = block_id // 2 - part_ref[0]
                place = jnp.where(side == 0, block_id % 2, jnp.where(side < 0, 2, 3))
            total[b, place] = total[b, place] + bits
    for b in range(blocks):
        for s in range(4):
            count_ref[b * block : (b + 1) * block, s * block : (s + 1) * block] = total[
                b, s
            ].astype(BF16)


def head_mixer():
    n = LANES
    row = lax.broadcasted_iota(jnp.int32, (2 * n, n), 0) % n
    lane = lax.broadcasted_iota(jnp.int32, (2 * n, n), 1)
    return jnp.where(row // 64 == lane // 64, 1.0 / 64, 0.0).astype(BF16)


def head_mean(value, mixer):
    high = value.astype(BF16)
    low = (value - high.astype(F32)).astype(BF16)
    return mul(jnp.concatenate([high, low], axis=1), mixer)


def head_lanes():
    first = lax.broadcasted_iota(jnp.int32, (1, LANES), 1) < 64
    ones = first.astype(F32)
    return first, [ones.astype(BF16), (1 - ones).astype(BF16)]


def own_kernel(
    scale_ref,
    x_ref,
    wq_ref,
    wk_ref,
    wv_ref,
    up_ref,
    count_ref,
    q_unit_ref,
    q_scale_ref,
    k_unit_ref,
    k_scale_ref,
    v_ref,
    e_ref,
    gw_ref,
    xt_ref,
    x_own,
):
    n = LANES
    for i in range(4):
        x_own[:, i * n : (i + 1) * n] = x_ref[i]
    x = x_own[...]
    xt_ref[...] = x.T
    mixer = head_mixer()
    first, heads = head_lanes()
    w_kv = jnp.concatenate([wk_ref[...], wv_ref[...]], axis=1)
    kv = mul(x, w_kv)
    q, k = mul(x, wq_ref[...]), kv[:, :n]
    q_scale = lax.rsqrt(head_mean(q * q, mixer) + EPS)
    k_scale = lax.rsqrt(head_mean(k * k, mixer) + EPS)
    q_unit, k_unit = q * q_scale, k * k_scale
    q_unit_ref[...], q_scale_ref[...] = q_unit, q_scale
    k_unit_ref[...], k_scale_ref[...] = k_unit, k_scale
    q_round, k_round, v_round = q_unit.astype(BF16), k_unit.astype(BF16), kv[:, n:].astype(BF16)
    v_ref[...] = v_round
    count = count_ref[:, : 2 * n].astype(F32)
    up = up_ref[...]
    for h in range(2):
        scores = mul(q_round * heads[h], k_round, NT) * (scale_ref[h] / 64)
        e_ref[h] = count * jnp.exp(scores)
        gw_ref[h] = mul(up * heads[h], v_round, NT)


def attend_kernel(
    part_ref,
    table_ref,
    scale_ref,
    xa_ref,
    xb_ref,
    wk_ref,
    wv_ref,
    up_ref,
    count_ref,
    q_unit_ref,
    q_scale_ref,
    k_unit_ref,
    k_scale_ref,
    v_ref,
    e_ref,
    gw_ref,
    xt_ref,
    att_ref,
    gq_ref,
    gown_ref,
    back_b_ref,
    keep_ref,
    away_ref,
    x_near,
    dw,
    wide,
    kv_near,
    q_stack,
    up_stack,
    gs_stack,
    w_stack,
):
    core, before, after = part_ref[0] % 2, table_ref[0, 0] % 2, table_ref[0, 1] % 2
    n = LANES

    @pl.when(core == 0)
    def _():
        for i in range(4):
            x_near[:n, i * n : (i + 1) * n] = xb_ref[i, pl.ds(before * n, n), :]
            x_near[n:, i * n : (i + 1) * n] = xa_ref[i, pl.ds(after * n, n), :]

    @pl.when(core != 0)
    def _():
        for i in range(4):
            x_near[:n, i * n : (i + 1) * n] = xa_ref[i, pl.ds(before * n, n), :]
            x_near[n:, i * n : (i + 1) * n] = xb_ref[i, pl.ds(after * n, n), :]

    mixer = head_mixer()
    first, heads = head_lanes()
    w_kv = jnp.concatenate([wk_ref[...], wv_ref[...]], axis=1)
    kv_near[...] = mul(x_near[...], w_kv)
    k = kv_near[:, :n]
    near_scale = lax.rsqrt(head_mean(k * k, mixer) + EPS)
    near_unit = k * near_scale
    k_near, v_near = near_unit.astype(BF16), kv_near[:, n:].astype(BF16)
    k_round = jnp.concatenate([k_unit_ref[...].astype(BF16), k_near], axis=0)
    v_round = jnp.concatenate([v_ref[...], v_near], axis=0)
    q_round, up = q_unit_ref[...].astype(BF16), up_ref[...]
    factors = [scale_ref[0] / 64, scale_ref[1] / 64]
    lane_factor = jnp.where(first, factors[0], factors[1])
    for b in range(2):
        at = slice(b * n, (b + 1) * n)
        count = count_ref[at, 2 * n :].astype(F32)
        for h in range(2):
            put = slice((2 * b + h) * n, (2 * b + h + 1) * n)
            q_h, up_h = q_round[at] * heads[h], up[at] * heads[h]
            q_stack[put], up_stack[put] = q_h, up_h
            far = count * jnp.exp(mul(q_h, k_near, NT) * factors[h])
            own = e_ref[h, at, :]
            total = jnp.sum(own[:, :n] + own[:, n:] + far[:, :n] + far[:, n:], axis=1, keepdims=True)
            inverse = 1.0 / total
            own, far = own * inverse, far * inverse
            gw_own, gw_far = gw_ref[h, at, :], mul(up_h, v_near, NT)
            own_d, far_d = own * gw_own, far * gw_far
            delta = jnp.sum(
                own_d[:, :n] + own_d[:, n:] + far_d[:, :n] + far_d[:, n:], axis=1, keepdims=True
            )
            w_stack[put, : 2 * n], w_stack[put, 2 * n :] = own.astype(BF16), far.astype(BF16)
            gs_stack[put, : 2 * n] = (own_d - own * delta).astype(BF16)
            gs_stack[put, 2 * n :] = (far_d - far * delta).astype(BF16)
    gqn = []
    for b in range(2):
        low, high = slice(2 * b * n, (2 * b + 1) * n), slice((2 * b + 1) * n, (2 * b + 2) * n)
        at = slice(b * n, (b + 1) * n)
        att = jnp.where(first, mul(w_stack[low], v_round), mul(w_stack[high], v_round))
        att_ref[at] = att.astype(BF16)
        gqn.append(jnp.where(first, mul(gs_stack[low], k_round), mul(gs_stack[high], k_round)))
    gqn = jnp.concatenate(gqn, axis=0) * lane_factor
    gkn = mul(q_stack[...], gs_stack[...], TN).T * lane_factor
    gv = mul(up_stack[...], w_stack[...], TN).T
    q_unit, q_scale = q_unit_ref[...], q_scale_ref[...]
    k_unit = jnp.concatenate([k_unit_ref[...], near_unit], axis=0)
    k_scale = jnp.concatenate([k_scale_ref[...], near_scale], axis=0)
    gq = (q_scale * (gqn - q_unit * head_mean(gqn * q_unit, mixer))).astype(BF16)
    gk = k_scale * (gkn - k_unit * head_mean(gkn * k_unit, mixer))
    gq_ref[...] = gq
    gown_ref[:, :n] = gk[: 2 * n]
    gown_ref[:, n:] = gv[: 2 * n]
    gk_round, gv_round = gk.astype(BF16), gv.astype(BF16)
    g_own = jnp.concatenate([gq, gk_round[: 2 * n], gv_round[: 2 * n]], axis=1)
    g_near = jnp.concatenate([gk_round[2 * n :], gv_round[2 * n :]], axis=1)
    dw[...] = mul(xt_ref[...], g_own)
    dw[:, n:] += mul(x_near[...], g_near, TN)
    for i in range(4):
        for ref, half in ((keep_ref, core), (wide, 1 - core)):
            rows = pl.ds(pl.multiple_of(half * 2 * n + i * 64, 64), 64)
            ref[0:64, i, : 3 * n] = dw[rows, :]
    wide[64] = jnp.full((4, 4 * n), jnp.where(core == 0, after, before), jnp.int32).astype(F32)
    back_b_ref[n:] = (
        jnp.full((16, 2 * n), jnp.where(core == 0, before, after), jnp.int32)
        .astype(F32)
        .astype(BF16)
    )

    def put_sides(near, other):
        for i in range(2):
            wide[0:64, i, 3 * n :] = gk[near + 64 * i : near + 64 * (i + 1)]
            wide[0:64, 2 + i, 3 * n :] = gv[near + 64 * i : near + 64 * (i + 1)]
        back_b_ref[:n, :n] = gk_round[other : other + n]
        back_b_ref[:n, n:] = gv_round[other : other + n]

    @pl.when(core == 0)
    def _():
        put_sides(3 * n, 2 * n)

    @pl.when(core != 0)
    def _():
        put_sides(2 * n, 3 * n)

    away_ref[...] = wide[...].astype(BF16)


def input_kernel(
    member_ref,
    gq_ref,
    gown_ref,
    swapped_ref,
    back_b_ref,
    wq_ref,
    wk_ref,
    wv_ref,
    own_ref,
    one_ref,
    two_ref,
    three_ref,
    wide,
    pieces,
):
    n = LANES
    wide[...] = swapped_ref[:, :, 3 * n :].astype(F32)
    near = jnp.concatenate(
        [
            jnp.concatenate([wide[0:64, i, :], wide[0:64, i + 1, :]], axis=0) for i in (0, 2)
        ],
        axis=1,
    )
    which = wide[64][:1]
    which = jnp.concatenate([which, which], axis=1)
    g = [gown_ref[:n] + near * (1 - which), gown_ref[n:] + near * which]
    body = back_b_ref[:n].astype(F32)
    which = back_b_ref[n : n + 16].astype(F32)[:1]
    g = [g[0] + body * (1 - which), g[1] + body * which]
    g = jnp.concatenate(g, axis=0).astype(BF16)
    part = mul(gq_ref[...], wq_ref[...], NT)
    part += mul(g[:, :n], wk_ref[...], NT)
    part += mul(g[:, n:], wv_ref[...], NT)
    for i in range(4):
        pieces[i] = part[:, i * n : (i + 1) * n]
    member = member_ref[0]
    own_ref[...] = pieces[member]
    for step, ref in enumerate((one_ref, two_ref, three_ref)):
        ref[...] = pieces[lax.rem(member + step + 1, 4)].astype(BF16)


def copies_kernel(value_ref, out_ref):
    for i in range(out_ref.shape[0]):
        out_ref[i] = value_ref[...]


def merge_kernel(keep_ref, swapped_ref, out_ref):
    width = keep_ref.shape[2]
    out_ref[...] = (keep_ref[...] + swapped_ref[0:64, :, :width].astype(F32)).astype(BF16)


def total_kernel(got_ref, out_ref):
    total = jnp.sum(got_ref[...].astype(F32), axis=0).astype(BF16)
    out_ref[...] = jnp.broadcast_to(total[None], out_ref.shape)


def add_kernel(own_ref, one_ref, two_ref, three_ref, out_ref):
    total = own_ref[...] + one_ref[...].astype(F32)
    total = total + two_ref[...].astype(F32) + three_ref[...].astype(F32)
    out_ref[...] = total.astype(BF16)


def final_kernel(grad_scale, mine_ref, gq_ref, gk_ref, gv_ref, wide):
    n = LANES
    wide[...] = mine_ref[...].astype(F32) * grad_scale
    for half in range(2):
        for i in range(4):
            rows = slice(half * 256 + i * 64, half * 256 + (i + 1) * 64)
            for j, out in enumerate((gq_ref, gk_ref, gv_ref)):
                out[rows, :] = wide[:, half, i, j * n : (j + 1) * n]


def shards(x, up, wq, wk, wv, scales, table, bitmap):
    parts = lax.axis_size("dom")
    part = lax.axis_index("dom")
    pairs = [(i, i ^ 1) for i in range(parts)]
    edges = [(i, i + 1) for i in range(1, parts - 1, 2)]
    edges = edges + [(b, a) for a, b in edges]

    members = lax.axis_size("mp")
    copies = call(copies_kernel, shape((members,) + x.shape, BF16), [VMEM], moved=400_000)(x)
    gathered = lax.all_to_all(copies, "mp", 0, 0, tiled=True)

    part_in = part.astype(jnp.int32).reshape(1)
    count = call(
        count_kernel,
        shape((256, 512), BF16),
        [SMEM, SMEM, VMEM],
        [pltpu.VMEM((2, 4, LANES, LANES), F32)],
        flops=2_000_000_000,
        moved=400_000,
    )(part_in, table, bitmap)

    gathered, count = lax.optimization_barrier((gathered, count))
    xa = lax.ppermute(gathered, "dom", pairs)
    xb = lax.ppermute(gathered, "dom", edges)
    tall = shape((256, 128), F32)
    square = shape((2, 256, 256), F32)
    own_parts = call(
        own_kernel,
        (tall, tall, tall, tall, shape((256, 128), BF16), square, square, shape((512, 256), BF16)),
        [SMEM] + [VMEM] * 6,
        [pltpu.VMEM((256, 512), BF16)],
        flops=3_000_000_000,
        moved=3_000_000,
    )(scales, gathered, wq, wk, wv, up, count)
    att, gq, gown, back_b, keep, away = call(
        attend_kernel,
        (
            shape((256, 128), BF16),
            shape((256, 128), BF16),
            shape((256, 256), F32),
            shape((144, 256), BF16),
            shape((64, 4, 384), F32),
            shape((65, 4, 512), BF16),
        ),
        [SMEM, SMEM, SMEM] + [VMEM] * 14,
        [
            pltpu.VMEM((256, 512), BF16),
            pltpu.VMEM((512, 384), F32),
            pltpu.VMEM((65, 4, 512), F32),
            pltpu.VMEM((256, 256), F32),
            pltpu.VMEM((512, 128), BF16),
            pltpu.VMEM((512, 128), BF16),
            pltpu.VMEM((512, 512), BF16),
            pltpu.VMEM((512, 512), BF16),
        ],
        flops=3_000_000_000,
        moved=4_000_000,
    )(part_in, table, scales, xa, xb, wk, wv, up, count, *own_parts)

    swapped = lax.ppermute(away, "dom", pairs)
    back_b = lax.ppermute(back_b, "dom", edges)
    pieces = call(merge_kernel, shape((64, 4, 384), BF16), [VMEM] * 2, moved=800_000)(
        keep, swapped
    )
    groups = [[2 * i + c for i in range(parts // 2)] for c in range(2)]
    got = lax.all_to_all(pieces, "dom", 0, 0, tiled=True, axis_index_groups=groups)
    totals = call(total_kernel, shape((128, 4, 384), BF16), [VMEM], moved=500_000)(got)
    totals, gown = lax.optimization_barrier((totals, gown))
    own, one, two, three = call(
        input_kernel,
        (shape((256, 128), F32),) + (shape((256, 128), BF16),) * 3,
        [SMEM] + [VMEM] * 7,
        [pltpu.VMEM((65, 4, 128), F32), pltpu.VMEM((4, 256, 128), F32)],
        flops=20_000_000_000,
        moved=1_500_000,
    )(lax.axis_index("mp").reshape(1), gq, gown, swapped, back_b, wq, wk, wv)
    one, two, three = (
        lax.ppermute(v, "mp", [(i, (i + s) % members) for i in range(members)])
        for s, v in ((1, one), (2, two), (3, three))
    )
    input_grad = call(
        add_kernel, shape((256, 128), BF16), [VMEM] * 4, moved=400_000
    )(own, one, two, three)
    mine = lax.all_to_all(totals, "dom", 0, 0, tiled=True)
    grad_scale = float(parts * 256) ** -0.5

    def finish(*refs):
        final_kernel(grad_scale, *refs)

    grads = call(
        finish,
        (shape((512, 128), F32),) * 3,
        [VMEM],
        [pltpu.VMEM((64, 2, 4, 384), F32)],
        moved=1_500_000,
    )(mine.reshape(64, 2, 4, 384))
    return (att, input_grad) + tuple(grads)


def solution(mesh):
    in_specs = (
        P("dom", "mp"),
        P("dom", "mp"),
        P(None, "mp"),
        P(None, "mp"),
        P(None, "mp"),
        P("mp"),
        P("dom", None),
        P("dom", None, None),
    )
    out_specs = (P("dom", "mp"), P("dom", "mp"), P(None, "mp"), P(None, "mp"), P(None, "mp"))
    return jax.shard_map(shards, mesh=mesh, in_specs=in_specs, out_specs=out_specs, check_vma=False)
```

```python
import jax
import jax.numpy as jnp
from jax import lax
from jax.experimental import pallas as pl
from jax.experimental.pallas import tpu as pltpu
from jax.sharding import PartitionSpec as P

EPS = 1e-06
F32 = jnp.float32
BF16 = jnp.bfloat16
LANES = 128
VMEM = pl.BlockSpec(memory_space=pltpu.VMEM)
SMEM = pl.BlockSpec(memory_space=pltpu.SMEM)
NN = (((1,), (0,)), ((), ()))
NT = (((1,), (1,)), ((), ()))
TN = (((0,), (0,)), ((), ()))


def mul(a, b, dims=NN):
    return lax.dot_general(a, b, dims, preferred_element_type=F32)


def call(kernel, out, in_specs, scratch=(), flops=0, moved=0):
    return pl.pallas_call(
        kernel,
        out_shape=out,
        in_specs=in_specs,
        out_specs=jax.tree.map(lambda _: VMEM, out),
        scratch_shapes=list(scratch),
        compiler_params=pltpu.CompilerParams(vmem_limit_bytes=40 * 1024 * 1024),
        cost_estimate=pl.CostEstimate(flops=flops, bytes_accessed=moved, transcendentals=0),
    )


def shape(dims, kind):
    return jax.ShapeDtypeStruct(dims, kind)


def count_kernel(part_ref, table_ref, words_ref, count_ref, total):
    blocks, tiles, words = words_ref.shape
    block = LANES
    per_row = words // block
    rows = block // per_row * 1
    total[...] = jnp.zeros_like(total)
    lane = lax.broadcasted_iota(jnp.int32, (block, block), 1)
    row = lax.broadcasted_iota(jnp.int32, (block, block), 0)
    same = (row % per_row) == (lane // 16)
    low_pick = jnp.where(same & (lane % 16 < 8), 1.0, 0.0)
    high_pick = jnp.where(same & (lane % 16 >= 8), 1.0, 0.0)
    pick = jnp.concatenate([low_pick, high_pick], axis=0).astype(BF16)
    mine = (row[:rows] == lane[:rows] // per_row).astype(F32)
    shift = lane % 8
    for b in range(blocks):
        for t in range(tiles):
            line = words_ref[b, t : t + 1, :]
            low = (line & 255).astype(F32)
            high = lax.shift_right_logical(line, 8).astype(F32)
            spread_rows = []
            for r in range(per_row):
                at = slice(r * block, (r + 1) * block)
                spread_rows.append(
                    jnp.concatenate([low[:, at] * mine, high[:, at] * mine], axis=1)
                )
            wide = jnp.concatenate(spread_rows, axis=0).astype(BF16)
            byte = mul(wide, pick).astype(jnp.int32)
            bits = (lax.shift_right_logical(byte, shift) & 1).astype(F32)
            place = b
            if t > 0:
                block_id = table_ref[b, t - 1]
                side = block_id // 2 - part_ref[0]
                place = jnp.where(side == 0, block_id % 2, jnp.where(side < 0, 2, 3))
            total[b, place] = total[b, place] + bits
    for b in range(blocks):
        for s in range(4):
            count_ref[b * block : (b + 1) * block, s * block : (s + 1) * block] = total[
                b, s
            ].astype(BF16)


def head_mixer():
    n = LANES
    row = lax.broadcasted_iota(jnp.int32, (2 * n, n), 0) % n
    lane = lax.broadcasted_iota(jnp.int32, (2 * n, n), 1)
    return jnp.where(row // 64 == lane // 64, 1.0 / 64, 0.0).astype(BF16)


def head_mean(value, mixer):
    high = value.astype(BF16)
    low = (value - high.astype(F32)).astype(BF16)
    return mul(jnp.concatenate([high, low], axis=1), mixer)


def head_lanes():
    first = lax.broadcasted_iota(jnp.int32, (1, LANES), 1) < 64
    ones = first.astype(F32)
    return first, [ones.astype(BF16), (1 - ones).astype(BF16)]


def own_kernel(
    scale_ref,
    x_ref,
    wq_ref,
    wk_ref,
    wv_ref,
    up_ref,
    count_ref,
    q_unit_ref,
    q_scale_ref,
    k_unit_ref,
    k_scale_ref,
    v_ref,
    e_ref,
    gw_ref,
    xt_ref,
    x_own,
):
    n = LANES
    for i in range(4):
        x_own[:, i * n : (i + 1) * n] = x_ref[i]
    x = x_own[...]
    xt_ref[...] = x.T
    mixer = head_mixer()
    first, heads = head_lanes()
    w_kv = jnp.concatenate([wk_ref[...], wv_ref[...]], axis=1)
    kv = mul(x, w_kv)
    q, k = mul(x, wq_ref[...]), kv[:, :n]
    q_scale = lax.rsqrt(head_mean(q * q, mixer) + EPS)
    k_scale = lax.rsqrt(head_mean(k * k, mixer) + EPS)
    q_unit, k_unit = q * q_scale, k * k_scale
    q_unit_ref[...], q_scale_ref[...] = q_unit, q_scale
    k_unit_ref[...], k_scale_ref[...] = k_unit, k_scale
    q_round, k_round, v_round = q_unit.astype(BF16), k_unit.astype(BF16), kv[:, n:].astype(BF16)
    v_ref[...] = v_round
    count = count_ref[:, : 2 * n].astype(F32)
    up = up_ref[...]
    for h in range(2):
        scores = mul(q_round * heads[h], k_round, NT) * (scale_ref[h] / 64)
        e_ref[h] = count * jnp.exp(scores)
        gw_ref[h] = mul(up * heads[h], v_round, NT)


def attend_kernel(
    part_ref,
    table_ref,
    scale_ref,
    xa_ref,
    xb_ref,
    wk_ref,
    wv_ref,
    up_ref,
    count_ref,
    q_unit_ref,
    q_scale_ref,
    k_unit_ref,
    k_scale_ref,
    v_ref,
    e_ref,
    gw_ref,
    xt_ref,
    att_ref,
    gq_ref,
    gown_ref,
    back_b_ref,
    keep_ref,
    away_ref,
    x_near,
    dw,
    wide,
    kv_near,
    q_stack,
    up_stack,
    gs_stack,
    w_stack,
):
    core, before, after = part_ref[0] % 2, table_ref[0, 0] % 2, table_ref[0, 1] % 2
    n = LANES

    @pl.when(core == 0)
    def _():
        for i in range(4):
            x_near[:n, i * n : (i + 1) * n] = xb_ref[i, pl.ds(before * n, n), :]
            x_near[n:, i * n : (i + 1) * n] = xa_ref[i, pl.ds(after * n, n), :]

    @pl.when(core != 0)
    def _():
        for i in range(4):
            x_near[:n, i * n : (i + 1) * n] = xa_ref[i, pl.ds(before * n, n), :]
            x_near[n:, i * n : (i + 1) * n] = xb_ref[i, pl.ds(after * n, n), :]

    mixer = head_mixer()
    first, heads = head_lanes()
    w_kv = jnp.concatenate([wk_ref[...], wv_ref[...]], axis=1)
    kv_near[...] = mul(x_near[...], w_kv)
    k = kv_near[:, :n]
    near_scale = lax.rsqrt(head_mean(k * k, mixer) + EPS)
    near_unit = k * near_scale
    k_near, v_near = near_unit.astype(BF16), kv_near[:, n:].astype(BF16)
    k_round = jnp.concatenate([k_unit_ref[...].astype(BF16), k_near], axis=0)
    v_round = jnp.concatenate([v_ref[...], v_near], axis=0)
    q_round, up = q_unit_ref[...].astype(BF16), up_ref[...]
    factors = [scale_ref[0] / 64, scale_ref[1] / 64]
    lane_factor = jnp.where(first, factors[0], factors[1])
    for b in range(2):
        at = slice(b * n, (b + 1) * n)
        count = count_ref[at, 2 * n :].astype(F32)
        for h in range(2):
            put = slice((2 * b + h) * n, (2 * b + h + 1) * n)
            q_h, up_h = q_round[at] * heads[h], up[at] * heads[h]
            q_stack[put], up_stack[put] = q_h, up_h
            far = count * jnp.exp(mul(q_h, k_near, NT) * factors[h])
            own = e_ref[h, at, :]
            total = jnp.sum(own[:, :n] + own[:, n:] + far[:, :n] + far[:, n:], axis=1, keepdims=True)
            inverse = 1.0 / total
            own, far = own * inverse, far * inverse
            gw_own, gw_far = gw_ref[h, at, :], mul(up_h, v_near, NT)
            own_d, far_d = own * gw_own, far * gw_far
            delta = jnp.sum(
                own_d[:, :n] + own_d[:, n:] + far_d[:, :n] + far_d[:, n:], axis=1, keepdims=True
            )
            w_stack[put, : 2 * n], w_stack[put, 2 * n :] = own.astype(BF16), far.astype(BF16)
            gs_stack[put, : 2 * n] = (own_d - own * delta).astype(BF16)
            gs_stack[put, 2 * n :] = (far_d - far * delta).astype(BF16)
    gqn = []
    for b in range(2):
        low, high = slice(2 * b * n, (2 * b + 1) * n), slice((2 * b + 1) * n, (2 * b + 2) * n)
        at = slice(b * n, (b + 1) * n)
        att = jnp.where(first, mul(w_stack[low], v_round), mul(w_stack[high], v_round))
        att_ref[at] = att.astype(BF16)
        gqn.append(jnp.where(first, mul(gs_stack[low], k_round), mul(gs_stack[high], k_round)))
    gqn = jnp.concatenate(gqn, axis=0) * lane_factor
    gkn = mul(q_stack[...], gs_stack[...], TN).T * lane_factor
    gv = mul(up_stack[...], w_stack[...], TN).T
    q_unit, q_scale = q_unit_ref[...], q_scale_ref[...]
    k_unit = jnp.concatenate([k_unit_ref[...], near_unit], axis=0)
    k_scale = jnp.concatenate([k_scale_ref[...], near_scale], axis=0)
    gq = (q_scale * (gqn - q_unit * head_mean(gqn * q_unit, mixer))).astype(BF16)
    gk = k_scale * (gkn - k_unit * head_mean(gkn * k_unit, mixer))
    gq_ref[...] = gq
    gown_ref[:, :n] = gk[: 2 * n]
    gown_ref[:, n:] = gv[: 2 * n]
    gk_round, gv_round = gk.astype(BF16), gv.astype(BF16)
    g_own = jnp.concatenate([gq, gk_round[: 2 * n], gv_round[: 2 * n]], axis=1)
    g_near = jnp.concatenate([gk_round[2 * n :], gv_round[2 * n :]], axis=1)
    dw[...] = mul(xt_ref[...], g_own)
    dw[:, n:] += mul(x_near[...], g_near, TN)
    for ref, half in ((keep_ref, core), (wide, 1 - core)):
        rows = pl.ds(pl.multiple_of(half * 2 * n, 2 * n), 2 * n)
        ref[0:64, :, : 3 * n] = dw[rows, :].reshape(64, 4, 3 * n)
    wide[64] = jnp.full((4, 4 * n), jnp.where(core == 0, after, before), jnp.int32).astype(F32)
    back_b_ref[n:] = (
        jnp.full((16, 2 * n), jnp.where(core == 0, before, after), jnp.int32)
        .astype(F32)
        .astype(BF16)
    )

    def put_sides(near, other):
        wide[0:32, :, 3 * n :] = gk[near : near + n].reshape(32, 4, n)
        wide[32:64, :, 3 * n :] = gv[near : near + n].reshape(32, 4, n)
        back_b_ref[:n, :n] = gk_round[other : other + n]
        back_b_ref[:n, n:] = gv_round[other : other + n]

    @pl.when(core == 0)
    def _():
        put_sides(3 * n, 2 * n)

    @pl.when(core != 0)
    def _():
        put_sides(2 * n, 3 * n)

    away_ref[...] = wide[...].astype(BF16)


def input_kernel(
    member_ref,
    gq_ref,
    gown_ref,
    swapped_ref,
    back_b_ref,
    wq_ref,
    wk_ref,
    wv_ref,
    own_ref,
    one_ref,
    two_ref,
    three_ref,
    wide,
    pieces,
):
    n = LANES
    wide[...] = swapped_ref[:, :, 3 * n :].astype(F32)
    near = jnp.concatenate(
        [wide[0:32].reshape(n, n), wide[32:64].reshape(n, n)], axis=1
    )
    which = wide[64][:1]
    which = jnp.concatenate([which, which], axis=1)
    g = [gown_ref[:n] + near * (1 - which), gown_ref[n:] + near * which]
    body = back_b_ref[:n].astype(F32)
    which = back_b_ref[n : n + 16].astype(F32)[:1]
    g = [g[0] + body * (1 - which), g[1] + body * which]
    g = jnp.concatenate(g, axis=0).astype(BF16)
    part = mul(gq_ref[...], wq_ref[...], NT)
    part += mul(g[:, :n], wk_ref[...], NT)
    part += mul(g[:, n:], wv_ref[...], NT)
    for i in range(4):
        pieces[i] = part[:, i * n : (i + 1) * n]
    member = member_ref[0]
    own_ref[...] = pieces[member]
    for step, ref in enumerate((one_ref, two_ref, three_ref)):
        ref[...] = pieces[lax.rem(member + step + 1, 4)].astype(BF16)


def copies_kernel(value_ref, out_ref):
    for i in range(out_ref.shape[0]):
        out_ref[i] = value_ref[...]


def merge_kernel(keep_ref, swapped_ref, out_ref):
    width = keep_ref.shape[2]
    out_ref[...] = (keep_ref[...] + swapped_ref[0:64, :, :width].astype(F32)).astype(BF16)


def total_kernel(got_ref, out_ref):
    total = jnp.sum(got_ref[...].astype(F32), axis=0).astype(BF16)
    out_ref[...] = jnp.broadcast_to(total[None], out_ref.shape)


def final_kernel(
    grad_scale,
    mine_ref,
    own_ref,
    one_ref,
    two_ref,
    three_ref,
    gq_ref,
    gk_ref,
    gv_ref,
    input_ref,
    wide,
):
    n = LANES
    total = own_ref[...] + one_ref[...].astype(F32)
    total = total + two_ref[...].astype(F32) + three_ref[...].astype(F32)
    input_ref[...] = total.astype(BF16)
    wide[...] = mine_ref[...].astype(F32) * grad_scale
    for half in range(2):
        for j, out in enumerate((gq_ref, gk_ref, gv_ref)):
            rows = slice(half * 2 * n, (half + 1) * 2 * n)
            out[rows, :] = wide[:, half, :, j * n : (j + 1) * n].reshape(2 * n, n)


def shards(x, up, wq, wk, wv, scales, table, bitmap):
    parts = lax.axis_size("dom")
    part = lax.axis_index("dom")
    pairs = [(i, i ^ 1) for i in range(parts)]
    edges = [(i, i + 1) for i in range(1, parts - 1, 2)]
    edges = edges + [(b, a) for a, b in edges]

    members = lax.axis_size("mp")
    copies = call(copies_kernel, shape((members,) + x.shape, BF16), [VMEM], moved=400_000)(x)
    gathered = lax.all_to_all(copies, "mp", 0, 0, tiled=True)

    part_in = part.astype(jnp.int32).reshape(1)
    count = call(
        count_kernel,
        shape((256, 512), BF16),
        [SMEM, SMEM, VMEM],
        [pltpu.VMEM((2, 4, LANES, LANES), F32)],
        flops=2_000_000_000,
        moved=400_000,
    )(part_in, table, bitmap)

    gathered, count = lax.optimization_barrier((gathered, count))
    xa = lax.ppermute(gathered, "dom", pairs)
    xb = lax.ppermute(gathered, "dom", edges)
    tall = shape((256, 128), F32)
    square = shape((2, 256, 256), F32)
    own_parts = call(
        own_kernel,
        (tall, tall, tall, tall, shape((256, 128), BF16), square, square, shape((512, 256), BF16)),
        [SMEM] + [VMEM] * 6,
        [pltpu.VMEM((256, 512), BF16)],
        flops=3_000_000_000,
        moved=3_000_000,
    )(scales, gathered, wq, wk, wv, up, count)
    att, gq, gown, back_b, keep, away = call(
        attend_kernel,
        (
            shape((256, 128), BF16),
            shape((256, 128), BF16),
            shape((256, 256), F32),
            shape((144, 256), BF16),
            shape((64, 4, 384), F32),
            shape((65, 4, 512), BF16),
        ),
        [SMEM, SMEM, SMEM] + [VMEM] * 14,
        [
            pltpu.VMEM((256, 512), BF16),
            pltpu.VMEM((512, 384), F32),
            pltpu.VMEM((65, 4, 512), F32),
            pltpu.VMEM((256, 256), F32),
            pltpu.VMEM((512, 128), BF16),
            pltpu.VMEM((512, 128), BF16),
            pltpu.VMEM((512, 512), BF16),
            pltpu.VMEM((512, 512), BF16),
        ],
        flops=3_000_000_000,
        moved=4_000_000,
    )(part_in, table, scales, xa, xb, wk, wv, up, count, *own_parts)

    swapped = lax.ppermute(away, "dom", pairs)
    back_b = lax.ppermute(back_b, "dom", edges)
    pieces = call(merge_kernel, shape((64, 4, 384), BF16), [VMEM] * 2, moved=800_000)(
        keep, swapped
    )
    groups = [[2 * i + c for i in range(parts // 2)] for c in range(2)]
    got = lax.all_to_all(pieces, "dom", 0, 0, tiled=True, axis_index_groups=groups)
    totals = call(total_kernel, shape((128, 4, 384), BF16), [VMEM], moved=500_000)(got)
    totals, gown = lax.optimization_barrier((totals, gown))
    own, one, two, three = call(
        input_kernel,
        (shape((256, 128), F32),) + (shape((256, 128), BF16),) * 3,
        [SMEM] + [VMEM] * 7,
        [pltpu.VMEM((65, 4, 128), F32), pltpu.VMEM((4, 256, 128), F32)],
        flops=20_000_000_000,
        moved=1_500_000,
    )(lax.axis_index("mp").reshape(1), gq, gown, swapped, back_b, wq, wk, wv)
    one, two, three = (
        lax.ppermute(v, "mp", [(i, (i + s) % members) for i in range(members)])
        for s, v in ((1, one), (2, two), (3, three))
    )
    mine = lax.all_to_all(totals, "dom", 0, 0, tiled=True)
    mine, one, two, three = lax.optimization_barrier((mine, one, two, three))
    grad_scale = float(parts * 256) ** -0.5

    def finish(*refs):
        final_kernel(grad_scale, *refs)

    *grads, input_grad = call(
        finish,
        (shape((512, 128), F32),) * 3 + (shape((256, 128), BF16),),
        [VMEM] * 5,
        [pltpu.VMEM((64, 2, 4, 384), F32)],
        moved=1_500_000,
    )(mine.reshape(64, 2, 4, 384), own, one, two, three)
    return (att, input_grad) + tuple(grads)


def solution(mesh):
    in_specs = (
        P("dom", "mp"),
        P("dom", "mp"),
        P(None, "mp"),
        P(None, "mp"),
        P(None, "mp"),
        P("mp"),
        P("dom", None),
        P("dom", None, None),
    )
    out_specs = (P("dom", "mp"), P("dom", "mp"), P(None, "mp"), P(None, "mp"), P(None, "mp"))
    return jax.shard_map(shards, mesh=mesh, in_specs=in_specs, out_specs=out_specs, check_vma=False)
```

```python
import jax
import jax.numpy as jnp
from jax import lax
from jax.experimental import pallas as pl
from jax.experimental.pallas import tpu as pltpu
from jax.sharding import PartitionSpec as P

EPS = 1e-06
F32 = jnp.float32
BF16 = jnp.bfloat16
LANES = 128
VMEM = pl.BlockSpec(memory_space=pltpu.VMEM)
SMEM = pl.BlockSpec(memory_space=pltpu.SMEM)
NN = (((1,), (0,)), ((), ()))
NT = (((1,), (1,)), ((), ()))
TN = (((0,), (0,)), ((), ()))


def mul(a, b, dims=NN):
    return lax.dot_general(a, b, dims, preferred_element_type=F32)


def call(kernel, out, in_specs, scratch=(), flops=0, moved=0):
    return pl.pallas_call(
        kernel,
        out_shape=out,
        in_specs=in_specs,
        out_specs=jax.tree.map(lambda _: VMEM, out),
        scratch_shapes=list(scratch),
        compiler_params=pltpu.CompilerParams(vmem_limit_bytes=40 * 1024 * 1024),
        cost_estimate=pl.CostEstimate(flops=flops, bytes_accessed=moved, transcendentals=0),
    )


def shape(dims, kind):
    return jax.ShapeDtypeStruct(dims, kind)


def count_kernel(part_ref, table_ref, words_ref, count_ref, total):
    blocks, tiles, words = words_ref.shape
    block = LANES
    per_row = words // block
    rows = block // per_row * 1
    total[...] = jnp.zeros_like(total)
    lane = lax.broadcasted_iota(jnp.int32, (block, block), 1)
    row = lax.broadcasted_iota(jnp.int32, (block, block), 0)
    same = (row % per_row) == (lane // 16)
    low_pick = jnp.where(same & (lane % 16 < 8), 1.0, 0.0)
    high_pick = jnp.where(same & (lane % 16 >= 8), 1.0, 0.0)
    pick = jnp.concatenate([low_pick, high_pick], axis=0).astype(BF16)
    mine = (row[:rows] == lane[:rows] // per_row).astype(F32)
    shift = lane % 8
    for b in range(blocks):
        for t in range(tiles):
            line = words_ref[b, t : t + 1, :]
            low = (line & 255).astype(F32)
            high = lax.shift_right_logical(line, 8).astype(F32)
            spread_rows = []
            for r in range(per_row):
                at = slice(r * block, (r + 1) * block)
                spread_rows.append(
                    jnp.concatenate([low[:, at] * mine, high[:, at] * mine], axis=1)
                )
            wide = jnp.concatenate(spread_rows, axis=0).astype(BF16)
            byte = mul(wide, pick).astype(jnp.int32)
            bits = (lax.shift_right_logical(byte, shift) & 1).astype(F32)
            place = b
            if t > 0:
                block_id = table_ref[b, t - 1]
                side = block_id // 2 - part_ref[0]
                place = jnp.where(side == 0, block_id % 2, jnp.where(side < 0, 2, 3))
            total[b, place] = total[b, place] + bits
    for b in range(blocks):
        for s in range(4):
            count_ref[b * block : (b + 1) * block, s * block : (s + 1) * block] = total[
                b, s
            ].astype(BF16)


def head_mixer():
    n = LANES
    row = lax.broadcasted_iota(jnp.int32, (2 * n, n), 0) % n
    lane = lax.broadcasted_iota(jnp.int32, (2 * n, n), 1)
    return jnp.where(row // 64 == lane // 64, 1.0 / 64, 0.0).astype(BF16)


def head_mean(value, mixer):
    high = value.astype(BF16)
    low = (value - high.astype(F32)).astype(BF16)
    return mul(jnp.concatenate([high, low], axis=1), mixer)


def head_lanes():
    first = lax.broadcasted_iota(jnp.int32, (1, LANES), 1) < 64
    ones = first.astype(F32)
    return first, [ones.astype(BF16), (1 - ones).astype(BF16)]


def own_kernel(
    scale_ref,
    x_ref,
    wq_ref,
    wk_ref,
    wv_ref,
    up_ref,
    count_ref,
    q_unit_ref,
    q_scale_ref,
    k_unit_ref,
    k_scale_ref,
    v_ref,
    e_ref,
    gw_ref,
    xt_ref,
    x_own,
):
    n = LANES
    for i in range(4):
        x_own[:, i * n : (i + 1) * n] = x_ref[i]
    x = x_own[...]
    xt_ref[...] = x.T
    mixer = head_mixer()
    first, heads = head_lanes()
    w_kv = jnp.concatenate([wk_ref[...], wv_ref[...]], axis=1)
    kv = mul(x, w_kv)
    q, k = mul(x, wq_ref[...]), kv[:, :n]
    q_scale = lax.rsqrt(head_mean(q * q, mixer) + EPS)
    k_scale = lax.rsqrt(head_mean(k * k, mixer) + EPS)
    q_unit, k_unit = q * q_scale, k * k_scale
    q_unit_ref[...], q_scale_ref[...] = q_unit, q_scale
    k_unit_ref[...], k_scale_ref[...] = k_unit, k_scale
    q_round, k_round, v_round = q_unit.astype(BF16), k_unit.astype(BF16), kv[:, n:].astype(BF16)
    v_ref[...] = v_round
    count = count_ref[:, : 2 * n].astype(F32)
    up = up_ref[...]
    for h in range(2):
        scores = mul(q_round * heads[h], k_round, NT) * (scale_ref[h] / 64)
        e_ref[h] = count * jnp.exp(scores)
        gw_ref[h] = mul(up * heads[h], v_round, NT)


def attend_kernel(
    part_ref,
    table_ref,
    scale_ref,
    xa_ref,
    xb_ref,
    wk_ref,
    wv_ref,
    up_ref,
    count_ref,
    q_unit_ref,
    q_scale_ref,
    k_unit_ref,
    k_scale_ref,
    v_ref,
    e_ref,
    gw_ref,
    xt_ref,
    w_stack,
    v_all_ref,
    gq_ref,
    gown_ref,
    back_b_ref,
    keep_ref,
    away_ref,
    x_near,
    kv_near,
    q_stack,
    up_stack,
    gs_stack,
):
    core, before, after = part_ref[0] % 2, table_ref[0, 0] % 2, table_ref[0, 1] % 2
    n = LANES

    @pl.when(core == 0)
    def _():
        for i in range(4):
            x_near[:n, i * n : (i + 1) * n] = xb_ref[i, pl.ds(before * n, n), :]
            x_near[n:, i * n : (i + 1) * n] = xa_ref[i, pl.ds(after * n, n), :]

    @pl.when(core != 0)
    def _():
        for i in range(4):
            x_near[:n, i * n : (i + 1) * n] = xa_ref[i, pl.ds(before * n, n), :]
            x_near[n:, i * n : (i + 1) * n] = xb_ref[i, pl.ds(after * n, n), :]

    mixer = head_mixer()
    first, heads = head_lanes()
    w_kv = jnp.concatenate([wk_ref[...], wv_ref[...]], axis=1)
    kv_near[...] = mul(x_near[...], w_kv)
    k = kv_near[:, :n]
    near_scale = lax.rsqrt(head_mean(k * k, mixer) + EPS)
    near_unit = k * near_scale
    k_near, v_near = near_unit.astype(BF16), kv_near[:, n:].astype(BF16)
    k_round = jnp.concatenate([k_unit_ref[...].astype(BF16), k_near], axis=0)
    v_round = jnp.concatenate([v_ref[...], v_near], axis=0)
    v_all_ref[...] = v_round
    q_round, up = q_unit_ref[...].astype(BF16), up_ref[...]
    factors = [scale_ref[0] / 64, scale_ref[1] / 64]
    lane_factor = jnp.where(first, factors[0], factors[1])
    for b in range(2):
        at = slice(b * n, (b + 1) * n)
        count = count_ref[at, 2 * n :].astype(F32)
        for h in range(2):
            put = slice((2 * b + h) * n, (2 * b + h + 1) * n)
            q_h, up_h = q_round[at] * heads[h], up[at] * heads[h]
            q_stack[put], up_stack[put] = q_h, up_h
            far = count * jnp.exp(mul(q_h, k_near, NT) * factors[h])
            own = e_ref[h, at, :]
            total = jnp.sum(own[:, :n] + own[:, n:] + far[:, :n] + far[:, n:], axis=1, keepdims=True)
            inverse = 1.0 / total
            own, far = own * inverse, far * inverse
            gw_own, gw_far = gw_ref[h, at, :], mul(up_h, v_near, NT)
            own_d, far_d = own * gw_own, far * gw_far
            delta = jnp.sum(
                own_d[:, :n] + own_d[:, n:] + far_d[:, :n] + far_d[:, n:], axis=1, keepdims=True
            )
            w_stack[put, : 2 * n], w_stack[put, 2 * n :] = own.astype(BF16), far.astype(BF16)
            gs_stack[put, : 2 * n] = (own_d - own * delta).astype(BF16)
            gs_stack[put, 2 * n :] = (far_d - far * delta).astype(BF16)
    gqn = []
    for b in range(2):
        low, high = slice(2 * b * n, (2 * b + 1) * n), slice((2 * b + 1) * n, (2 * b + 2) * n)
        gqn.append(jnp.where(first, mul(gs_stack[low], k_round), mul(gs_stack[high], k_round)))
    gqn = jnp.concatenate(gqn, axis=0) * lane_factor
    gkn = mul(q_stack[...], gs_stack[...], TN).T * lane_factor
    gv = mul(up_stack[...], w_stack[...], TN).T
    q_unit, q_scale = q_unit_ref[...], q_scale_ref[...]
    k_unit = jnp.concatenate([k_unit_ref[...], near_unit], axis=0)
    k_scale = jnp.concatenate([k_scale_ref[...], near_scale], axis=0)
    gq = (q_scale * (gqn - q_unit * head_mean(gqn * q_unit, mixer))).astype(BF16)
    gk = k_scale * (gkn - k_unit * head_mean(gkn * k_unit, mixer))
    gq_ref[...] = gq
    gown_ref[:, :n] = gk[: 2 * n]
    gown_ref[:, n:] = gv[: 2 * n]
    gk_round, gv_round = gk.astype(BF16), gv.astype(BF16)
    g_own = jnp.concatenate([gq, gk_round[: 2 * n], gv_round[: 2 * n]], axis=1)
    g_near = jnp.concatenate([gk_round[2 * n :], gv_round[2 * n :]], axis=1)
    for half, ref in ((core, keep_ref), (1 - core, away_ref)):
        at = pl.ds(pl.multiple_of(half * 2 * n, 2 * n), 2 * n)
        dw = mul(xt_ref[at, :], g_own)
        far = mul(x_near[:, at], g_near, TN)
        dw = jnp.concatenate([dw[:, :n], dw[:, n:] + far], axis=1)
        ref[0:64, :, : 3 * n] = dw.reshape(64, 4, 3 * n).astype(ref.dtype)
    which = jnp.full((4, 4 * n), jnp.where(core == 0, after, before), jnp.int32)
    away_ref[64] = which.astype(F32).astype(BF16)
    back_b_ref[n:] = (
        jnp.full((16, 2 * n), jnp.where(core == 0, before, after), jnp.int32)
        .astype(F32)
        .astype(BF16)
    )

    def put_sides(near, other):
        away_ref[0:32, :, 3 * n :] = gk[near : near + n].reshape(32, 4, n).astype(BF16)
        away_ref[32:64, :, 3 * n :] = gv[near : near + n].reshape(32, 4, n).astype(BF16)
        back_b_ref[:n, :n] = gk_round[other : other + n]
        back_b_ref[:n, n:] = gv_round[other : other + n]

    @pl.when(core == 0)
    def _():
        put_sides(3 * n, 2 * n)

    @pl.when(core != 0)
    def _():
        put_sides(2 * n, 3 * n)


def input_kernel(
    member_ref,
    w_ref,
    v_ref,
    gq_ref,
    gown_ref,
    swapped_ref,
    back_b_ref,
    wq_ref,
    wk_ref,
    wv_ref,
    att_ref,
    own_ref,
    one_ref,
    two_ref,
    three_ref,
    wide,
    pieces,
):
    n = LANES
    wide[...] = swapped_ref[:, :, 3 * n :].astype(F32)
    near = jnp.concatenate(
        [wide[0:32].reshape(n, n), wide[32:64].reshape(n, n)], axis=1
    )
    which = wide[64][:1]
    which = jnp.concatenate([which, which], axis=1)
    g = [gown_ref[:n] + near * (1 - which), gown_ref[n:] + near * which]
    body = back_b_ref[:n].astype(F32)
    which = back_b_ref[n : n + 16].astype(F32)[:1]
    g = [g[0] + body * (1 - which), g[1] + body * which]
    g = jnp.concatenate(g, axis=0).astype(BF16)
    part = mul(gq_ref[...], wq_ref[...], NT)
    part += mul(g[:, :n], wk_ref[...], NT)
    part += mul(g[:, n:], wv_ref[...], NT)
    for i in range(4):
        pieces[i] = part[:, i * n : (i + 1) * n]
    first, _ = head_lanes()
    v_all = v_ref[...]
    for b in range(2):
        low, high = slice(2 * b * n, (2 * b + 1) * n), slice((2 * b + 1) * n, (2 * b + 2) * n)
        att = jnp.where(first, mul(w_ref[low], v_all), mul(w_ref[high], v_all))
        att_ref[b * n : (b + 1) * n] = att.astype(BF16)
    member = member_ref[0]
    own_ref[...] = pieces[member]
    for step, ref in enumerate((one_ref, two_ref, three_ref)):
        ref[...] = pieces[lax.rem(member + step + 1, 4)].astype(BF16)


def copies_kernel(value_ref, out_ref):
    for i in range(out_ref.shape[0]):
        out_ref[i] = value_ref[...]


def merge_kernel(keep_ref, swapped_ref, out_ref):
    width = keep_ref.shape[2]
    out_ref[...] = (keep_ref[...] + swapped_ref[0:64, :, :width].astype(F32)).astype(BF16)


def total_kernel(got_ref, out_ref):
    total = jnp.sum(got_ref[...].astype(F32), axis=0).astype(BF16)
    out_ref[...] = jnp.broadcast_to(total[None], out_ref.shape)


def final_kernel(
    grad_scale,
    mine_ref,
    own_ref,
    one_ref,
    two_ref,
    three_ref,
    gq_ref,
    gk_ref,
    gv_ref,
    input_ref,
    wide,
):
    n = LANES
    total = own_ref[...] + one_ref[...].astype(F32)
    total = total + two_ref[...].astype(F32) + three_ref[...].astype(F32)
    input_ref[...] = total.astype(BF16)
    wide[...] = mine_ref[...].astype(F32) * grad_scale
    for half in range(2):
        for j, out in enumerate((gq_ref, gk_ref, gv_ref)):
            rows = slice(half * 2 * n, (half + 1) * 2 * n)
            out[rows, :] = wide[:, half, :, j * n : (j + 1) * n].reshape(2 * n, n)


def shards(x, up, wq, wk, wv, scales, table, bitmap):
    parts = lax.axis_size("dom")
    part = lax.axis_index("dom")
    pairs = [(i, i ^ 1) for i in range(parts)]
    edges = [(i, i + 1) for i in range(1, parts - 1, 2)]
    edges = edges + [(b, a) for a, b in edges]

    members = lax.axis_size("mp")
    copies = call(copies_kernel, shape((members,) + x.shape, BF16), [VMEM], moved=400_000)(x)
    gathered = lax.all_to_all(copies, "mp", 0, 0, tiled=True)

    part_in = part.astype(jnp.int32).reshape(1)
    count = call(
        count_kernel,
        shape((256, 512), BF16),
        [SMEM, SMEM, VMEM],
        [pltpu.VMEM((2, 4, LANES, LANES), F32)],
        flops=2_000_000_000,
        moved=400_000,
    )(part_in, table, bitmap)

    gathered, count = lax.optimization_barrier((gathered, count))
    xa = lax.ppermute(gathered, "dom", pairs)
    xb = lax.ppermute(gathered, "dom", edges)
    tall = shape((256, 128), F32)
    square = shape((2, 256, 256), F32)
    own_parts = call(
        own_kernel,
        (tall, tall, tall, tall, shape((256, 128), BF16), square, square, shape((512, 256), BF16)),
        [SMEM] + [VMEM] * 6,
        [pltpu.VMEM((256, 512), BF16)],
        flops=3_000_000_000,
        moved=3_000_000,
    )(scales, gathered, wq, wk, wv, up, count)
    w_all, v_all, gq, gown, back_b, keep, away = call(
        attend_kernel,
        (
            shape((512, 512), BF16),
            shape((512, 128), BF16),
            shape((256, 128), BF16),
            shape((256, 256), F32),
            shape((144, 256), BF16),
            shape((64, 4, 384), F32),
            shape((65, 4, 512), BF16),
        ),
        [SMEM, SMEM, SMEM] + [VMEM] * 14,
        [
            pltpu.VMEM((256, 512), BF16),
            pltpu.VMEM((256, 256), F32),
            pltpu.VMEM((512, 128), BF16),
            pltpu.VMEM((512, 128), BF16),
            pltpu.VMEM((512, 512), BF16),
        ],
        flops=3_000_000_000,
        moved=4_000_000,
    )(part_in, table, scales, xa, xb, wk, wv, up, count, *own_parts)

    swapped = lax.ppermute(away, "dom", pairs)
    back_b = lax.ppermute(back_b, "dom", edges)
    pieces = call(merge_kernel, shape((64, 4, 384), BF16), [VMEM] * 2, moved=800_000)(
        keep, swapped
    )
    groups = [[2 * i + c for i in range(parts // 2)] for c in range(2)]
    got = lax.all_to_all(pieces, "dom", 0, 0, tiled=True, axis_index_groups=groups)
    totals = call(total_kernel, shape((128, 4, 384), BF16), [VMEM], moved=500_000)(got)
    totals, gown = lax.optimization_barrier((totals, gown))
    att, own, one, two, three = call(
        input_kernel,
        (shape((256, 128), BF16), shape((256, 128), F32)) + (shape((256, 128), BF16),) * 3,
        [SMEM] + [VMEM] * 9,
        [pltpu.VMEM((65, 4, 128), F32), pltpu.VMEM((4, 256, 128), F32)],
        flops=20_000_000_000,
        moved=1_500_000,
    )(lax.axis_index("mp").reshape(1), w_all, v_all, gq, gown, swapped, back_b, wq, wk, wv)
    one, two, three = (
        lax.ppermute(v, "mp", [(i, (i + s) % members) for i in range(members)])
        for s, v in ((1, one), (2, two), (3, three))
    )
    mine = lax.all_to_all(totals, "dom", 0, 0, tiled=True)
    mine, one, two, three = lax.optimization_barrier((mine, one, two, three))
    grad_scale = float(parts * 256) ** -0.5

    def finish(*refs):
        final_kernel(grad_scale, *refs)

    *grads, input_grad = call(
        finish,
        (shape((512, 128), F32),) * 3 + (shape((256, 128), BF16),),
        [VMEM] * 5,
        [pltpu.VMEM((64, 2, 4, 384), F32)],
        moved=1_500_000,
    )(mine.reshape(64, 2, 4, 384), own, one, two, three)
    return (att, input_grad) + tuple(grads)


def solution(mesh):
    in_specs = (
        P("dom", "mp"),
        P("dom", "mp"),
        P(None, "mp"),
        P(None, "mp"),
        P(None, "mp"),
        P("mp"),
        P("dom", None),
        P("dom", None, None),
    )
    out_specs = (P("dom", "mp"), P("dom", "mp"), P(None, "mp"), P(None, "mp"), P(None, "mp"))
    return jax.shard_map(shards, mesh=mesh, in_specs=in_specs, out_specs=out_specs, check_vma=False)
```

```python
import jax
import jax.numpy as jnp
from jax import lax
from jax.experimental import pallas as pl
from jax.experimental.pallas import tpu as pltpu
from jax.sharding import PartitionSpec as P

EPS = 1e-06
F32 = jnp.float32
BF16 = jnp.bfloat16
LANES = 128
VMEM = pl.BlockSpec(memory_space=pltpu.VMEM)
SMEM = pl.BlockSpec(memory_space=pltpu.SMEM)
NN = (((1,), (0,)), ((), ()))
NT = (((1,), (1,)), ((), ()))
TN = (((0,), (0,)), ((), ()))


def mul(a, b, dims=NN):
    return lax.dot_general(a, b, dims, preferred_element_type=F32)


def call(kernel, out, in_specs, scratch=(), flops=0, moved=0):
    return pl.pallas_call(
        kernel,
        out_shape=out,
        in_specs=in_specs,
        out_specs=jax.tree.map(lambda _: VMEM, out),
        scratch_shapes=list(scratch),
        compiler_params=pltpu.CompilerParams(vmem_limit_bytes=40 * 1024 * 1024),
        cost_estimate=pl.CostEstimate(flops=flops, bytes_accessed=moved, transcendentals=0),
    )


def shape(dims, kind):
    return jax.ShapeDtypeStruct(dims, kind)


def count_kernel(part_ref, table_ref, words_ref, count_ref, total):
    blocks, tiles, words = words_ref.shape
    block = LANES
    per_row = words // block
    rows = block // per_row * 1
    total[...] = jnp.zeros_like(total)
    lane = lax.broadcasted_iota(jnp.int32, (block, block), 1)
    row = lax.broadcasted_iota(jnp.int32, (block, block), 0)
    same = (row % per_row) == (lane // 16)
    low_pick = jnp.where(same & (lane % 16 < 8), 1.0, 0.0)
    high_pick = jnp.where(same & (lane % 16 >= 8), 1.0, 0.0)
    pick = jnp.concatenate([low_pick, high_pick], axis=0).astype(BF16)
    mine = (row[:rows] == lane[:rows] // per_row).astype(F32)
    shift = lane % 8
    for b in range(blocks):
        for t in range(tiles):
            line = words_ref[b, t : t + 1, :]
            low = (line & 255).astype(F32)
            high = lax.shift_right_logical(line, 8).astype(F32)
            spread_rows = []
            for r in range(per_row):
                at = slice(r * block, (r + 1) * block)
                spread_rows.append(
                    jnp.concatenate([low[:, at] * mine, high[:, at] * mine], axis=1)
                )
            wide = jnp.concatenate(spread_rows, axis=0).astype(BF16)
            byte = mul(wide, pick).astype(jnp.int32)
            bits = (lax.shift_right_logical(byte, shift) & 1).astype(F32)
            place = b
            if t > 0:
                block_id = table_ref[b, t - 1]
                side = block_id // 2 - part_ref[0]
                place = jnp.where(side == 0, block_id % 2, jnp.where(side < 0, 2, 3))
            total[b, place] = total[b, place] + bits
    for b in range(blocks):
        for s in range(4):
            count_ref[b * block : (b + 1) * block, s * block : (s + 1) * block] = total[
                b, s
            ].astype(BF16)


def head_mixer():
    n = LANES
    row = lax.broadcasted_iota(jnp.int32, (2 * n, n), 0) % n
    lane = lax.broadcasted_iota(jnp.int32, (2 * n, n), 1)
    return jnp.where(row // 64 == lane // 64, 1.0 / 64, 0.0).astype(BF16)


def head_mean(value, mixer):
    high = value.astype(BF16)
    low = (value - high.astype(F32)).astype(BF16)
    return mul(jnp.concatenate([high, low], axis=1), mixer)


def head_lanes():
    first = lax.broadcasted_iota(jnp.int32, (1, LANES), 1) < 64
    ones = first.astype(F32)
    return first, [ones.astype(BF16), (1 - ones).astype(BF16)]


def own_kernel(
    scale_ref,
    x_ref,
    wq_ref,
    wk_ref,
    wv_ref,
    up_ref,
    count_ref,
    q_unit_ref,
    q_scale_ref,
    k_unit_ref,
    k_scale_ref,
    v_ref,
    e_ref,
    gw_ref,
    xt_ref,
    x_own,
):
    n = LANES
    for i in range(4):
        x_own[:, i * n : (i + 1) * n] = x_ref[i]
    x = x_own[...]
    xt_ref[...] = x.T
    mixer = head_mixer()
    first, heads = head_lanes()
    w_kv = jnp.concatenate([wk_ref[...], wv_ref[...]], axis=1)
    kv = mul(x, w_kv)
    q, k = mul(x, wq_ref[...]), kv[:, :n]
    q_scale = lax.rsqrt(head_mean(q * q, mixer) + EPS)
    k_scale = lax.rsqrt(head_mean(k * k, mixer) + EPS)
    q_unit, k_unit = q * q_scale, k * k_scale
    q_unit_ref[...], q_scale_ref[...] = q_unit, q_scale
    k_unit_ref[...], k_scale_ref[...] = k_unit, k_scale
    q_round, k_round, v_round = q_unit.astype(BF16), k_unit.astype(BF16), kv[:, n:].astype(BF16)
    v_ref[...] = v_round
    count = count_ref[:, : 2 * n].astype(F32)
    up = up_ref[...]
    for h in range(2):
        scores = mul(q_round * heads[h], k_round, NT) * (scale_ref[h] / 64)
        e_ref[h] = count * jnp.exp(scores)
        gw_ref[h] = mul(up * heads[h], v_round, NT)


def attend_kernel(
    part_ref,
    table_ref,
    scale_ref,
    xa_ref,
    xb_ref,
    wk_ref,
    wv_ref,
    up_ref,
    count_ref,
    q_unit_ref,
    q_scale_ref,
    k_unit_ref,
    k_scale_ref,
    v_ref,
    e_ref,
    gw_ref,
    xt_ref,
    w_stack,
    v_all_ref,
    gq_ref,
    gown_ref,
    back_b_ref,
    keep_ref,
    away_ref,
    x_near,
    kv_near,
    q_stack,
    up_stack,
    gs_stack,
):
    core, before, after = part_ref[0] % 2, table_ref[0, 0] % 2, table_ref[0, 1] % 2
    n = LANES

    @pl.when(core == 0)
    def _():
        for i in range(4):
            x_near[:n, i * n : (i + 1) * n] = xb_ref[i, pl.ds(before * n, n), :]
            x_near[n:, i * n : (i + 1) * n] = xa_ref[i, pl.ds(after * n, n), :]

    @pl.when(core != 0)
    def _():
        for i in range(4):
            x_near[:n, i * n : (i + 1) * n] = xa_ref[i, pl.ds(before * n, n), :]
            x_near[n:, i * n : (i + 1) * n] = xb_ref[i, pl.ds(after * n, n), :]

    mixer = head_mixer()
    first, heads = head_lanes()
    w_kv = jnp.concatenate([wk_ref[...], wv_ref[...]], axis=1)
    kv_near[...] = mul(x_near[...], w_kv)
    k = kv_near[:, :n]
    near_scale = lax.rsqrt(head_mean(k * k, mixer) + EPS)
    near_unit = k * near_scale
    k_near, v_near = near_unit.astype(BF16), kv_near[:, n:].astype(BF16)
    k_round = jnp.concatenate([k_unit_ref[...].astype(BF16), k_near], axis=0)
    v_round = jnp.concatenate([v_ref[...], v_near], axis=0)
    v_all_ref[...] = v_round
    q_round, up = q_unit_ref[...].astype(BF16), up_ref[...]
    factors = [scale_ref[0] / 64, scale_ref[1] / 64]
    lane_factor = jnp.where(first, factors[0], factors[1])
    for b in range(2):
        at = slice(b * n, (b + 1) * n)
        count = count_ref[at, 2 * n :].astype(F32)
        for h in range(2):
            put = slice((2 * b + h) * n, (2 * b + h + 1) * n)
            q_h, up_h = q_round[at] * heads[h], up[at] * heads[h]
            q_stack[put], up_stack[put] = q_h, up_h
            far = count * jnp.exp(mul(q_h, k_near, NT) * factors[h])
            own = e_ref[h, at, :]
            total = jnp.sum(own[:, :n] + own[:, n:] + far[:, :n] + far[:, n:], axis=1, keepdims=True)
            inverse = 1.0 / total
            own, far = own * inverse, far * inverse
            gw_own, gw_far = gw_ref[h, at, :], mul(up_h, v_near, NT)
            own_d, far_d = own * gw_own, far * gw_far
            delta = jnp.sum(
                own_d[:, :n] + own_d[:, n:] + far_d[:, :n] + far_d[:, n:], axis=1, keepdims=True
            )
            w_stack[put, : 2 * n], w_stack[put, 2 * n :] = own.astype(BF16), far.astype(BF16)
            gs_stack[put, : 2 * n] = (own_d - own * delta).astype(BF16)
            gs_stack[put, 2 * n :] = (far_d - far * delta).astype(BF16)
    gqn = []
    for b in range(2):
        low, high = slice(2 * b * n, (2 * b + 1) * n), slice((2 * b + 1) * n, (2 * b + 2) * n)
        gqn.append(jnp.where(first, mul(gs_stack[low], k_round), mul(gs_stack[high], k_round)))
    gqn = jnp.concatenate(gqn, axis=0) * lane_factor
    gkn = mul(q_stack[...], gs_stack[...], TN).T * lane_factor
    gv = mul(up_stack[...], w_stack[...], TN).T
    q_unit, q_scale = q_unit_ref[...], q_scale_ref[...]
    k_unit = jnp.concatenate([k_unit_ref[...], near_unit], axis=0)
    k_scale = jnp.concatenate([k_scale_ref[...], near_scale], axis=0)
    gq = (q_scale * (gqn - q_unit * head_mean(gqn * q_unit, mixer))).astype(BF16)
    gk = k_scale * (gkn - k_unit * head_mean(gkn * k_unit, mixer))
    gq_ref[...] = gq
    gown_ref[:, :n] = gk[: 2 * n]
    gown_ref[:, n:] = gv[: 2 * n]
    gk_round, gv_round = gk.astype(BF16), gv.astype(BF16)
    g_own = jnp.concatenate([gq, gk_round[: 2 * n], gv_round[: 2 * n]], axis=1)
    g_near = jnp.concatenate([gk_round[2 * n :], gv_round[2 * n :]], axis=1)
    for half, ref in ((core, keep_ref), (1 - core, away_ref)):
        at = pl.ds(pl.multiple_of(half * 2 * n, 2 * n), 2 * n)
        dw = mul(xt_ref[at, :], g_own)
        far = mul(x_near[:, at], g_near, TN)
        dw = jnp.concatenate([dw[:, :n], dw[:, n:] + far], axis=1)
        ref[0:64, :, : 3 * n] = dw.reshape(64, 4, 3 * n).astype(ref.dtype)
    which = jnp.full((4, 4 * n), jnp.where(core == 0, after, before), jnp.int32)
    away_ref[64] = which.astype(F32).astype(BF16)
    back_b_ref[n:] = (
        jnp.full((16, 2 * n), jnp.where(core == 0, before, after), jnp.int32)
        .astype(F32)
        .astype(BF16)
    )

    def put_sides(near, other):
        away_ref[0:32, :, 3 * n :] = gk[near : near + n].reshape(32, 4, n).astype(BF16)
        away_ref[32:64, :, 3 * n :] = gv[near : near + n].reshape(32, 4, n).astype(BF16)
        back_b_ref[:n, :n] = gk_round[other : other + n]
        back_b_ref[:n, n:] = gv_round[other : other + n]

    @pl.when(core == 0)
    def _():
        put_sides(3 * n, 2 * n)

    @pl.when(core != 0)
    def _():
        put_sides(2 * n, 3 * n)


def attended_kernel(w_ref, v_ref, att_ref):
    n = LANES
    first, _ = head_lanes()
    v_all = v_ref[...]
    for b in range(2):
        low, high = slice(2 * b * n, (2 * b + 1) * n), slice((2 * b + 1) * n, (2 * b + 2) * n)
        att = jnp.where(first, mul(w_ref[low], v_all), mul(w_ref[high], v_all))
        att_ref[b * n : (b + 1) * n] = att.astype(BF16)


def input_kernel(
    member_ref,
    gq_ref,
    gown_ref,
    swapped_ref,
    back_b_ref,
    wq_ref,
    wk_ref,
    wv_ref,
    own_ref,
    one_ref,
    two_ref,
    three_ref,
    wide,
    pieces,
):
    n = LANES
    wide[...] = swapped_ref[:, :, 3 * n :].astype(F32)
    near = jnp.concatenate(
        [wide[0:32].reshape(n, n), wide[32:64].reshape(n, n)], axis=1
    )
    which = wide[64][:1]
    which = jnp.concatenate([which, which], axis=1)
    g = [gown_ref[:n] + near * (1 - which), gown_ref[n:] + near * which]
    body = back_b_ref[:n].astype(F32)
    which = back_b_ref[n : n + 16].astype(F32)[:1]
    g = [g[0] + body * (1 - which), g[1] + body * which]
    g = jnp.concatenate(g, axis=0).astype(BF16)
    part = mul(gq_ref[...], wq_ref[...], NT)
    part += mul(g[:, :n], wk_ref[...], NT)
    part += mul(g[:, n:], wv_ref[...], NT)
    for i in range(4):
        pieces[i] = part[:, i * n : (i + 1) * n]
    member = member_ref[0]
    own_ref[...] = pieces[member]
    for step, ref in enumerate((one_ref, two_ref, three_ref)):
        ref[...] = pieces[lax.rem(member + step + 1, 4)].astype(BF16)


def copies_kernel(value_ref, out_ref):
    for i in range(out_ref.shape[0]):
        out_ref[i] = value_ref[...]


def merge_kernel(keep_ref, swapped_ref, out_ref):
    width = keep_ref.shape[2]
    out_ref[...] = (keep_ref[...] + swapped_ref[0:64, :, :width].astype(F32)).astype(BF16)


def total_kernel(got_ref, out_ref):
    total = jnp.sum(got_ref[...].astype(F32), axis=0).astype(BF16)
    out_ref[...] = jnp.broadcast_to(total[None], out_ref.shape)


def final_kernel(
    grad_scale,
    mine_ref,
    own_ref,
    one_ref,
    two_ref,
    three_ref,
    gq_ref,
    gk_ref,
    gv_ref,
    input_ref,
    wide,
):
    n = LANES
    total = own_ref[...] + one_ref[...].astype(F32)
    total = total + two_ref[...].astype(F32) + three_ref[...].astype(F32)
    input_ref[...] = total.astype(BF16)
    wide[...] = mine_ref[...].astype(F32) * grad_scale
    for half in range(2):
        for j, out in enumerate((gq_ref, gk_ref, gv_ref)):
            rows = slice(half * 2 * n, (half + 1) * 2 * n)
            out[rows, :] = wide[:, half, :, j * n : (j + 1) * n].reshape(2 * n, n)


def shards(x, up, wq, wk, wv, scales, table, bitmap):
    parts = lax.axis_size("dom")
    part = lax.axis_index("dom")
    pairs = [(i, i ^ 1) for i in range(parts)]
    edges = [(i, i + 1) for i in range(1, parts - 1, 2)]
    edges = edges + [(b, a) for a, b in edges]

    members = lax.axis_size("mp")
    copies = call(copies_kernel, shape((members,) + x.shape, BF16), [VMEM], moved=400_000)(x)
    gathered = lax.all_to_all(copies, "mp", 0, 0, tiled=True)

    part_in = part.astype(jnp.int32).reshape(1)
    count = call(
        count_kernel,
        shape((256, 512), BF16),
        [SMEM, SMEM, VMEM],
        [pltpu.VMEM((2, 4, LANES, LANES), F32)],
        flops=2_000_000_000,
        moved=400_000,
    )(part_in, table, bitmap)

    gathered, count = lax.optimization_barrier((gathered, count))
    xa = lax.ppermute(gathered, "dom", pairs)
    xb = lax.ppermute(gathered, "dom", edges)
    tall = shape((256, 128), F32)
    square = shape((2, 256, 256), F32)
    own_parts = call(
        own_kernel,
        (tall, tall, tall, tall, shape((256, 128), BF16), square, square, shape((512, 256), BF16)),
        [SMEM] + [VMEM] * 6,
        [pltpu.VMEM((256, 512), BF16)],
        flops=3_000_000_000,
        moved=3_000_000,
    )(scales, gathered, wq, wk, wv, up, count)
    w_all, v_all, gq, gown, back_b, keep, away = call(
        attend_kernel,
        (
            shape((512, 512), BF16),
            shape((512, 128), BF16),
            shape((256, 128), BF16),
            shape((256, 256), F32),
            shape((144, 256), BF16),
            shape((64, 4, 384), F32),
            shape((65, 4, 512), BF16),
        ),
        [SMEM, SMEM, SMEM] + [VMEM] * 14,
        [
            pltpu.VMEM((256, 512), BF16),
            pltpu.VMEM((256, 256), F32),
            pltpu.VMEM((512, 128), BF16),
            pltpu.VMEM((512, 128), BF16),
            pltpu.VMEM((512, 512), BF16),
        ],
        flops=3_000_000_000,
        moved=4_000_000,
    )(part_in, table, scales, xa, xb, wk, wv, up, count, *own_parts)

    swapped = lax.ppermute(away, "dom", pairs)
    back_b = lax.ppermute(back_b, "dom", edges)
    pieces = call(merge_kernel, shape((64, 4, 384), BF16), [VMEM] * 2, moved=800_000)(
        keep, swapped
    )
    groups = [[2 * i + c for i in range(parts // 2)] for c in range(2)]
    pieces, w_all = lax.optimization_barrier((pieces, w_all))
    att = call(
        attended_kernel,
        shape((256, 128), BF16),
        [VMEM] * 2,
        flops=500_000_000,
        moved=800_000,
    )(w_all, v_all)
    got = lax.all_to_all(pieces, "dom", 0, 0, tiled=True, axis_index_groups=groups)
    got, att = lax.optimization_barrier((got, att))
    totals = call(total_kernel, shape((128, 4, 384), BF16), [VMEM], moved=500_000)(got)
    totals, gown = lax.optimization_barrier((totals, gown))
    own, one, two, three = call(
        input_kernel,
        (shape((256, 128), F32),) + (shape((256, 128), BF16),) * 3,
        [SMEM] + [VMEM] * 7,
        [pltpu.VMEM((65, 4, 128), F32), pltpu.VMEM((4, 256, 128), F32)],
        flops=20_000_000_000,
        moved=1_500_000,
    )(lax.axis_index("mp").reshape(1), gq, gown, swapped, back_b, wq, wk, wv)
    one, two, three = (
        lax.ppermute(v, "mp", [(i, (i + s) % members) for i in range(members)])
        for s, v in ((1, one), (2, two), (3, three))
    )
    mine = lax.all_to_all(totals, "dom", 0, 0, tiled=True)
    mine, one, two, three = lax.optimization_barrier((mine, one, two, three))
    grad_scale = float(parts * 256) ** -0.5

    def finish(*refs):
        final_kernel(grad_scale, *refs)

    *grads, input_grad = call(
        finish,
        (shape((512, 128), F32),) * 3 + (shape((256, 128), BF16),),
        [VMEM] * 5,
        [pltpu.VMEM((64, 2, 4, 384), F32)],
        moved=1_500_000,
    )(mine.reshape(64, 2, 4, 384), own, one, two, three)
    return (att, input_grad) + tuple(grads)


def solution(mesh):
    in_specs = (
        P("dom", "mp"),
        P("dom", "mp"),
        P(None, "mp"),
        P(None, "mp"),
        P(None, "mp"),
        P("mp"),
        P("dom", None),
        P("dom", None, None),
    )
    out_specs = (P("dom", "mp"), P("dom", "mp"), P(None, "mp"), P(None, "mp"), P(None, "mp"))
    return jax.shard_map(shards, mesh=mesh, in_specs=in_specs, out_specs=out_specs, check_vma=False)
```
